32 devices in a mesh: col: 8 (over y, x, core), row: 4 (over z).
Axes of the slice: x: 2, y: 2, z: 4, core: 2. Of those that a mesh axis runs over, the one named last changes fastest.
Arguments:
- kernel: float32 [512, 1024, 256], P('row', 'col'), may hold values from -0.01171875 to 0.01171875
- history: float32 [1024, 16, 256], P(('col', 'row')), may hold values from -6 to 6
- noise_weight: float32 [512, 256], P('row'), may hold values from 0.3 to 3
- prior_weight: float32 [1024], P(('col', 'row')), may hold values from 0.3 to 3
Outputs:
- hessian_action: float32 [1024, 16, 256], P(('col', 'row'))
The draws below stay inside these ranges and needn't reach their ends.
All inputs are finite; a program needn't handle non-finite values.
Results may differ from the reference program's by a relative error of at most 0.00005.
Values sent between devices are 32-bit elements; how exact they have to be, the bound alone decides.
A program may use at most 192 MiB of HBM per device.

```python
import math
import jax
import jax.numpy as jnp

S = 512
NT = 256
R = 16
P_SIZE = 1024


def levels(own_key, dims, cuts, low, high):
    factor_of = 1.0
    for position, blocks in cuts:
        steps = jax.random.uniform(jax.random.fold_in(jax.random.fold_in(own_key, 6), position), (blocks,), jnp.float32, low / len(cuts), high / len(cuts))
        factor_of = factor_of * jnp.repeat(jnp.exp(steps), dims[position] // blocks).reshape((-1,) + (1,) * (len(dims) - 1 - position))
    return factor_of


def scatter_about(key, extent, deviation, most, pieces=(), kind=jnp.bfloat16):
    factor_of = levels(key, extent, pieces, -0.22, 0.18) if pieces else 1.0
    array = jax.random.normal(key, extent, jnp.float32) * deviation * factor_of
    return jnp.minimum(jnp.maximum(array, -most), most).astype(kind)


def setup_inputs(seed: int = 0) -> dict:
    seeds = jax.random.split(jax.random.key(seed), 5)
    kernel = scatter_about(seeds[0], (S, P_SIZE, NT), (P_SIZE * NT) ** -0.5, 0.01171875, ((0, 4), (1, 8)), jnp.float32)
    history = scatter_about(seeds[1], (P_SIZE, R, NT), 1.0, 6.0, ((0, 32),), jnp.float32)
    noise_weight = jnp.clip(jnp.exp(math.log(3.0) - 2.3025851 * jax.random.uniform(seeds[2], (S, NT), jnp.float32) ** levels(seeds[2], (S, NT), ((0, 4),), -0.2, 0.2)), 0.3, 3.0)
    prior_weight = jnp.clip(jnp.exp(math.log(3.0) - 2.3025851 * jax.random.uniform(seeds[3], (P_SIZE,), jnp.float32) ** levels(seeds[3], (P_SIZE,), ((0, 32),), -0.2, 0.2)), 0.3, 3.0)
    return dict(kernel=kernel, history=history, noise_weight=noise_weight, prior_weight=prior_weight)


def reference(kernel, history, noise_weight, prior_weight):
    steps_total = history.shape[2]
    length = 2 * steps_total
    kernel_hat = jnp.fft.rfft(kernel, n=length, axis=2)
    history_hat = jnp.fft.rfft(history, n=length, axis=2)
    data_hat = jnp.einsum('spf,prf->srf', kernel_hat, history_hat)
    data = jnp.fft.irfft(data_hat, n=length, axis=2)[:, :, :steps_total]
    weighted = data * noise_weight[:, None, :]
    weighted_hat = jnp.fft.rfft(weighted, n=length, axis=2)
    gradient_hat = jnp.einsum('spf,srf->prf', jnp.conj(kernel_hat), weighted_hat)
    gradient = jnp.fft.irfft(gradient_hat, n=length, axis=2)[:, :, :steps_total]
    result = gradient + prior_weight[:, None, None] * history
    return result.astype(jnp.float32)
```

```python
import functools
import math

import jax
import jax.numpy as jnp
import ml_dtypes
import numpy as np
from jax import lax
from jax.experimental import pallas as pl
from jax.experimental.pallas import tpu as pltpu
from jax.sharding import PartitionSpec as P

f32 = jnp.float32
bf16 = jnp.bfloat16
VMEM_LIMIT = 48 * 1024 * 1024
SENSOR_BLOCK = 16
FREQ_BLOCK = 16


def transform_table(steps):
    freqs = np.arange(steps, dtype=np.int64)[:, None]
    times = np.arange(steps, dtype=np.int64)[None, :]
    phase = ((2 * freqs + 1) * times % (4 * steps)).astype(np.float64) * (math.pi / (2 * steps))
    return np.concatenate([np.cos(phase), -np.sin(phase)], axis=0)


def split_host(table):
    table = table.astype(np.float32)
    high = table.astype(ml_dtypes.bfloat16)
    low = (table - high.astype(np.float32)).astype(ml_dtypes.bfloat16)
    return high, low


def split(value):
    high = value.astype(bf16)
    return high, (value - high.astype(f32)).astype(bf16)


def matmul(lhs, rhs):
    return lax.dot_general(lhs, rhs, (((1,), (0,)), ((), ())), preferred_element_type=f32)


def matmul_nt(lhs, rhs):
    return lax.dot_general(lhs, rhs, (((1,), (1,)), ((), ())), preferred_element_type=f32)


def kernel_transform(table_ref, kernel_ref, out_ref, real_ref, imag_ref):
    sensors, params, steps = kernel_ref.shape
    for s in range(0, sensors, 2):
        high, low = split(kernel_ref[s : s + 2].reshape(2 * params, steps))
        spec = matmul_nt(table_ref[...], jnp.concatenate([high, low, high], axis=1))
        for j in range(2):
            cols = slice(j * params, (j + 1) * params)
            real_ref[pl.ds(s + j, steps, stride=sensors), :] = spec[:steps, cols]
            imag_ref[pl.ds(s + j, steps, stride=sensors), :] = spec[steps:, cols]

    group = 8

    def emit(i, carry):
        rows = pl.ds(pl.multiple_of(i * group * sensors, group * sensors), group * sensors)
        freqs = pl.ds(i * group, group)
        for part, ref in enumerate((real_ref, imag_ref)):
            high, low = split(ref[rows, :].reshape(group, sensors, params))
            out_ref[freqs, 0, :, part * params : (part + 1) * params] = high
            out_ref[freqs, 1, :, part * params : (part + 1) * params] = low
        return carry

    lax.fori_loop(0, steps // group, emit, 0)


def forward(table_ref, inverse_ref, hist_ref, khat_ref, out_ref, hreal_ref, himag_ref, data_ref):
    step = pl.program_id(0)
    blocks, vectors, part_params, steps = hist_ref.shape
    params = blocks * part_params
    freq_block, _, sensors, _ = khat_ref.shape

    @pl.when(step == 0)
    def _():
        for r in range(0, vectors, 2):
            hist = jnp.concatenate([hist_ref[:, r + j].reshape(params, steps) for j in range(2)], axis=0)
            high, low = split(hist)
            spec = matmul_nt(table_ref[...], jnp.concatenate([high, low, high], axis=1))
            for j in range(2):
                cols = slice(j * params, (j + 1) * params)
                hreal_ref[pl.ds(r + j, steps, stride=vectors), :] = spec[:steps, cols]
                himag_ref[pl.ds(r + j, steps, stride=vectors), :] = spec[steps:, cols]

    for i in range(freq_block):
        f = step * freq_block + i
        rows = pl.ds(pl.multiple_of(f * vectors, vectors), vectors)
        real, imag = hreal_ref[rows, :], himag_ref[rows, :]
        both = jnp.concatenate(
            [jnp.concatenate([real, -imag], axis=1), jnp.concatenate([imag, real], axis=1)], axis=0
        )
        lhs = jnp.concatenate(split(both), axis=0)
        res = matmul_nt(lhs, khat_ref[i].reshape(2 * sensors, 2 * params))
        top, bottom = res[: 2 * vectors], res[2 * vectors :]
        data_ref[pl.ds(pl.multiple_of(f * 2 * vectors, 2 * vectors), 2 * vectors), :] = (
            top[:, :sensors] + (top[:, sensors:] + bottom[:, :sensors])
        )

    @pl.when(step == pl.num_programs(0) - 1)
    def _():
        for r in range(0, vectors, 2):
            spec = jnp.concatenate(
                [
                    jnp.concatenate(
                        [data_ref[pl.ds(part * vectors + r + j, steps, stride=2 * vectors), :] for j in range(2)],
                        axis=1,
                    )
                    for part in range(2)
                ],
                axis=0,
            )
            high, low = split(spec)
            times = matmul(inverse_ref[...], jnp.concatenate([high, low, high], axis=0))
            for j in range(2):
                out_ref[r + j] = times[:, j * sensors : (j + 1) * sensors]


def adjoint(table_ref, inverse_ref, data_ref, noise_ref, khat_ref, out_ref, spec_ref, grad_ref):
    step = pl.program_id(0)
    vectors, steps, sensors = data_ref.shape
    freq_block, params = khat_ref.shape[0], khat_ref.shape[3] // 2
    blocks, _, part_params, _ = out_ref.shape

    @pl.when(step == 0)
    def _():
        for r in range(0, vectors, 2):
            weighted = jnp.concatenate([data_ref[r + j] * noise_ref[...] for j in range(2)], axis=1)
            high, low = split(weighted)
            spec = matmul(table_ref[...], jnp.concatenate([high, low, high], axis=0))
            for j in range(2):
                cols = slice(j * sensors, (j + 1) * sensors)
                spec_ref[pl.ds(r + j, steps, stride=2 * vectors), :] = spec[:steps, cols]
                spec_ref[pl.ds(vectors + r + j, steps, stride=2 * vectors), :] = spec[steps:, cols]

    for i in range(freq_block):
        f = step * freq_block + i
        base = pl.multiple_of(f * 2 * vectors, 2 * vectors)
        high, low = split(spec_ref[pl.ds(base, 2 * vectors), :])
        lhs = jnp.concatenate(
            [jnp.concatenate([high, high], axis=1), jnp.concatenate([low, jnp.zeros_like(low)], axis=1)], axis=0
        )
        res = matmul(lhs, khat_ref[i].reshape(2 * sensors, 2 * params))
        res = res[: 2 * vectors] + res[2 * vectors :]
        grad_ref[pl.ds(base, vectors), :] = res[:vectors, :params] + res[vectors:, params:]
        grad_ref[pl.ds(base + vectors, vectors), :] = res[vectors:, :params] - res[:vectors, params:]

    @pl.when(step == pl.num_programs(0) - 1)
    def _():
        for r in range(0, vectors, 2):
            spec = jnp.concatenate(
                [
                    jnp.concatenate(
                        [grad_ref[pl.ds(part * vectors + r + j, steps, stride=2 * vectors), :] for part in range(2)],
                        axis=0,
                    ).T
                    for j in range(2)
                ],
                axis=0,
            )
            high, low = split(spec)
            times = matmul(jnp.concatenate([high, low, high], axis=1), inverse_ref[...])
            for j in range(2):
                out_ref[:, r + j] = times[j * params : (j + 1) * params].reshape(blocks, part_params, steps)


def local(row_count, kernel, history, noise_weight, prior_weight):
    sensors, params, steps = kernel.shape
    part_params, vectors, _ = history.shape
    pad = -sensors % 128
    if pad:
        kernel = jnp.pad(kernel, ((0, pad), (0, 0), (0, 0)))
        noise_weight = jnp.pad(noise_weight, ((0, pad), (0, 0)))
        sensors += pad

    table = transform_table(steps)
    th, tl = split_host(table)
    ih, il = split_host(table / steps)
    table_k = jnp.asarray(np.concatenate([th, th, tl], axis=1))
    inverse_t = jnp.asarray(np.concatenate([ih.T, ih.T, il.T], axis=1))
    inverse_f = jnp.asarray(np.concatenate([ih, ih, il], axis=0))

    whole = lambda *shape: pl.BlockSpec(shape, lambda i: (0,) * len(shape))
    params_of = pltpu.CompilerParams(vmem_limit_bytes=VMEM_LIMIT)

    moved = history.transpose(1, 0, 2)
    gathered = lax.all_gather(moved, "row", axis=0)

    khat = pl.pallas_call(
        kernel_transform,
        grid=(sensors // SENSOR_BLOCK,),
        in_specs=[
            whole(2 * steps, 3 * steps),
            pl.BlockSpec((SENSOR_BLOCK, params, steps), lambda i: (i, 0, 0)),
        ],
        out_specs=pl.BlockSpec((steps, 2, SENSOR_BLOCK, 2 * params), lambda i: (0, 0, i, 0)),
        out_shape=jax.ShapeDtypeStruct((steps, 2, sensors, 2 * params), bf16),
        scratch_shapes=[pltpu.VMEM((steps * SENSOR_BLOCK, params), f32)] * 2,
        compiler_params=params_of,
        cost_estimate=pl.CostEstimate(
            flops=12 * sensors * params * steps * steps,
            bytes_accessed=12 * sensors * params * steps,
            transcendentals=0,
        ),
        name="kernel_transform",
    )(table_k, kernel)

    khat_spec = pl.BlockSpec((FREQ_BLOCK, 2, sensors, 2 * params), lambda i: (i, 0, 0, 0))
    freq_cost = pl.CostEstimate(
        flops=16 * vectors * sensors * params * steps,
        bytes_accessed=8 * sensors * params * steps,
        transcendentals=0,
    )
    partial = pl.pallas_call(
        forward,
        grid=(steps // FREQ_BLOCK,),
        in_specs=[
            whole(2 * steps, 3 * steps),
            whole(steps, 6 * steps),
            whole(row_count, vectors, part_params, steps),
            khat_spec,
        ],
        out_specs=whole(vectors, steps, sensors),
        out_shape=jax.ShapeDtypeStruct((vectors, steps, sensors), f32),
        scratch_shapes=[
            pltpu.VMEM((steps * vectors, params), f32),
            pltpu.VMEM((steps * vectors, params), f32),
            pltpu.VMEM((steps * 2 * vectors, sensors), f32),
        ],
        compiler_params=params_of,
        cost_estimate=freq_cost,
        name="forward",
    )(table_k, inverse_t, gathered, khat)

    data = lax.psum(partial, "col")

    grad = pl.pallas_call(
        adjoint,
        grid=(steps // FREQ_BLOCK,),
        in_specs=[
            whole(2 * steps, 3 * steps),
            whole(6 * steps, steps),
            whole(vectors, steps, sensors),
            whole(steps, sensors),
            khat_spec,
        ],
        out_specs=whole(row_count, vectors, part_params, steps),
        out_shape=jax.ShapeDtypeStruct((row_count, vectors, part_params, steps), f32),
        scratch_shapes=[
            pltpu.VMEM((steps * 2 * vectors, sensors), f32),
            pltpu.VMEM((steps * 2 * vectors, params), f32),
        ],
        compiler_params=params_of,
        cost_estimate=freq_cost,
        name="adjoint",
    )(table_k, inverse_f, data, noise_weight.T, khat)

    gradient = lax.psum_scatter(grad, "row", scatter_dimension=0, tiled=False)
    return gradient.transpose(1, 0, 2) + prior_weight[:, None, None] * history


def solution(mesh):
    in_specs = (
        P("row", "col", None),
        P(("col", "row"), None, None),
        P("row", None),
        P(("col", "row")),
    )
    out_specs = P(("col", "row"), None, None)
    return jax.shard_map(
        functools.partial(local, mesh.shape["row"]),
        mesh=mesh,
        in_specs=in_specs,
        out_specs=out_specs,
        check_vma=False,
    )
```

```python
import functools
import math

import jax
import jax.numpy as jnp
import ml_dtypes
import numpy as np
from jax import lax
from jax.experimental import pallas as pl
from jax.experimental.pallas import tpu as pltpu
from jax.sharding import PartitionSpec as P

f32 = jnp.float32
bf16 = jnp.bfloat16
VMEM_LIMIT = 48 * 1024 * 1024
SENSOR_BLOCK = 16
FREQ_BLOCK = 16


def transform_table(steps):
    freqs = np.arange(steps, dtype=np.int64)[:, None]
    times = np.arange(steps, dtype=np.int64)[None, :]
    phase = ((2 * freqs + 1) * times % (4 * steps)).astype(np.float64) * (math.pi / (2 * steps))
    return np.concatenate([np.cos(phase), -np.sin(phase)], axis=0)


def split_host(table):
    table = table.astype(np.float32)
    high = table.astype(ml_dtypes.bfloat16)
    low = (table - high.astype(np.float32)).astype(ml_dtypes.bfloat16)
    return high, low


def split(value):
    high = value.astype(bf16)
    return high, (value - high.astype(f32)).astype(bf16)


def matmul(lhs, rhs):
    return lax.dot_general(lhs, rhs, (((1,), (0,)), ((), ())), preferred_element_type=f32)


def matmul_nt(lhs, rhs):
    return lax.dot_general(lhs, rhs, (((1,), (1,)), ((), ())), preferred_element_type=f32)


def kernel_transform(table_ref, kernel_ref, out_ref, real_ref, imag_ref):
    sensors, params, steps = kernel_ref.shape
    for s in range(0, sensors, 2):
        high, low = split(kernel_ref[s : s + 2].reshape(2 * params, steps))
        spec = matmul_nt(table_ref[...], jnp.concatenate([high, low, high], axis=1))
        for j in range(2):
            cols = slice(j * params, (j + 1) * params)
            real_ref[pl.ds(s + j, steps, stride=sensors), :] = spec[:steps, cols]
            imag_ref[pl.ds(s + j, steps, stride=sensors), :] = spec[steps:, cols]

    group = 8

    def emit(i, carry):
        rows = pl.ds(pl.multiple_of(i * group * sensors, group * sensors), group * sensors)
        freqs = pl.ds(i * group, group)
        for part, ref in enumerate((real_ref, imag_ref)):
            high, low = split(ref[rows, :].reshape(group, sensors, params))
            out_ref[freqs, 0, :, part * params : (part + 1) * params] = high
            out_ref[freqs, 1, :, part * params : (part + 1) * params] = low
        return carry

    lax.fori_loop(0, steps // group, emit, 0)


MESH = pl.DeviceIdType.MESH


def col_steps(bits):
    rest = list(range(1, bits))
    return [rest, rest[::-1]]


def normal_operator(
    bits,
    table_k_ref,
    inverse_t_ref,
    inverse_f_ref,
    hist_ref,
    noise_ref,
    khat_ref,
    out_ref,
    hreal_ref,
    himag_ref,
    spec_ref,
    grad_ref,
    time_ref,
    weighted_ref,
    *comm,
):
    recv_refs, (send_sem, recv_sem) = comm[:-2], comm[-2:]
    step = pl.program_id(0)
    half_steps = pl.num_programs(0) // 2
    blocks, vectors, part_params, steps = hist_ref.shape
    params = blocks * part_params
    freq_block, _, sensors, _ = khat_ref.shape
    total = vectors * steps
    me = lax.axis_index("col")
    bit_of = [lax.rem(me // 2**b, 2) for b in range(bits)]
    partner = [me + (1 - 2 * bit_of[b]) * 2**b for b in range(bits)]
    orders = col_steps(bits)

    @pl.when(step == 0)
    def _():
        barrier = pltpu.get_barrier_semaphore()
        for b in range(bits):
            pl.semaphore_signal(barrier, inc=1, device_id={"col": partner[b]}, device_id_type=MESH)
        pl.semaphore_wait(barrier, bits)

        for r in range(0, vectors, 2):
            hist = jnp.concatenate([hist_ref[:, r + j].reshape(params, steps) for j in range(2)], axis=0)
            high, low = split(hist)
            spec = matmul_nt(table_k_ref[...], jnp.concatenate([high, low, high], axis=1))
            for j in range(2):
                cols = slice(j * params, (j + 1) * params)
                hreal_ref[pl.ds(r + j, steps, stride=vectors), :] = spec[:steps, cols]
                himag_ref[pl.ds(r + j, steps, stride=vectors), :] = spec[steps:, cols]

    @pl.when(step < half_steps)
    def _():
        for i in range(freq_block):
            f = step * freq_block + i
            rows = pl.ds(pl.multiple_of(f * vectors, vectors), vectors)
            real, imag = hreal_ref[rows, :], himag_ref[rows, :]
            both = jnp.concatenate(
                [jnp.concatenate([real, -imag], axis=1), jnp.concatenate([imag, real], axis=1)], axis=0
            )
            lhs = jnp.concatenate(split(both), axis=0)
            res = matmul_nt(lhs, khat_ref[i].reshape(2 * sensors, 2 * params))
            top, bottom = res[: 2 * vectors], res[2 * vectors :]
            spec_ref[pl.ds(pl.multiple_of(f * 2 * vectors, 2 * vectors), 2 * vectors), :] = (
                top[:, :sensors] + (top[:, sensors:] + bottom[:, :sensors])
            )

    def to_time(r):
        spec = jnp.concatenate(
            [
                jnp.concatenate(
                    [spec_ref[pl.ds(part * vectors + r + j, steps, stride=2 * vectors), :] for j in range(2)],
                    axis=1,
                )
                for part in range(2)
            ],
            axis=0,
        )
        high, low = split(spec)
        times = matmul(inverse_t_ref[...], jnp.concatenate([high, low, high], axis=0))
        for j in range(2):
            rows = pl.ds(pl.multiple_of((r + j) * steps, steps), steps)
            time_ref[rows, :] = times[:, j * sensors : (j + 1) * sensors]

    def to_spectrum(r):
        rows = [pl.ds(pl.multiple_of((r + j) * steps, steps), steps) for j in range(2)]
        high, low = split(jnp.concatenate([weighted_ref[rows[j], :] for j in range(2)], axis=1))
        spec = matmul(table_k_ref[...], jnp.concatenate([high, low, high], axis=0))
        for j in range(2):
            cols = slice(j * sensors, (j + 1) * sensors)
            spec_ref[pl.ds(r + j, steps, stride=2 * vectors), :] = spec[:steps, cols]
            spec_ref[pl.ds(vectors + r + j, steps, stride=2 * vectors), :] = spec[steps:, cols]

    @pl.when(step == half_steps - 1)
    def _():
        def rows_of(offset, length):
            return pl.ds(pl.multiple_of(offset, 8), length)

        def exchange(src, dst, sem, bit):
            copy = pltpu.make_async_remote_copy(
                src_ref=src,
                dst_ref=dst,
                send_sem=send_sem.at[sem],
                recv_sem=recv_sem.at[sem],
                device_id={"col": partner[bit]},
                device_id_type=MESH,
            )
            copy.start()
            return copy

        half = vectors // 2
        keep, give = bit_of[0] * half, (1 - bit_of[0]) * half

        def give_body(j, carry):
            to_time(give + 2 * j)
            return carry

        def keep_body(j, carry):
            to_time(keep + 2 * j)
            return carry

        lax.fori_loop(0, half // 2, give_body, 0)
        length = total // 2
        first = exchange(time_ref.at[rows_of(give * steps, length)], recv_refs[0], 0, 0)
        lax.fori_loop(0, half // 2, keep_body, 0)
        first.wait()

        length //= 2
        offsets = [keep * steps, keep * steps + length]
        for part in range(2):
            rows = rows_of(offsets[part], length)
            time_ref[rows, :] += recv_refs[0][part * length : (part + 1) * length, :]
        sem = 1
        for level in range(bits - 1):
            length //= 2
            copies = []
            for part in range(2):
                bit = orders[part][level]
                send_at = offsets[part] + (1 - bit_of[bit]) * length
                offsets[part] = offsets[part] + bit_of[bit] * length
                copies.append(exchange(time_ref.at[rows_of(send_at, length)], recv_refs[sem], sem, bit))
                sem += 1
            for part in range(2):
                copies[part].wait()
                rows = rows_of(offsets[part], length)
                time_ref[rows, :] += recv_refs[sem - 2 + part][...]

        piece = min(length, steps)
        for part in range(2):
            for j in range(length // piece):
                at = offsets[part] + j * piece
                noise = noise_ref[rows_of(lax.rem(at, steps), piece), :]
                weighted_ref[rows_of(at, piece), :] = time_ref[rows_of(at, piece), :] * noise

        for level in reversed(range(bits - 1)):
            copies = []
            for part in range(2):
                bit = orders[part][level]
                rows = weighted_ref.at[rows_of(offsets[part], length)]
                copies.append(exchange(rows, rows, sem, bit))
                sem += 1
            for part in range(2):
                copies[part].wait()
                offsets[part] = offsets[part] - bit_of[orders[part][level]] * length
            length *= 2
        rows = weighted_ref.at[rows_of(keep * steps, 2 * length)]
        last = exchange(rows, rows, sem, 0)

        def keep_spectrum(j, carry):
            to_spectrum(keep + 2 * j)
            return carry

        def give_spectrum(j, carry):
            to_spectrum(give + 2 * j)
            return carry

        lax.fori_loop(0, half // 2, keep_spectrum, 0)
        last.wait()
        lax.fori_loop(0, half // 2, give_spectrum, 0)

    @pl.when(step >= half_steps)
    def _():
        for i in range(freq_block):
            f = (step - half_steps) * freq_block + i
            base = pl.multiple_of(f * 2 * vectors, 2 * vectors)
            high, low = split(spec_ref[pl.ds(base, 2 * vectors), :])
            lhs = jnp.concatenate(
                [jnp.concatenate([high, high], axis=1), jnp.concatenate([low, jnp.zeros_like(low)], axis=1)], axis=0
            )
            res = matmul(lhs, khat_ref[i].reshape(2 * sensors, 2 * params))
            res = res[: 2 * vectors] + res[2 * vectors :]
            grad_ref[pl.ds(base, vectors), :] = res[:vectors, :params] + res[vectors:, params:]
            grad_ref[pl.ds(base + vectors, vectors), :] = res[vectors:, :params] - res[:vectors, params:]

    @pl.when(step == 2 * half_steps - 1)
    def _():
        for r in range(0, vectors, 2):
            spec = jnp.concatenate(
                [
                    jnp.concatenate(
                        [grad_ref[pl.ds(part * vectors + r + j, steps, stride=2 * vectors), :] for part in range(2)],
                        axis=0,
                    ).T
                    for j in range(2)
                ],
                axis=0,
            )
            high, low = split(spec)
            times = matmul(jnp.concatenate([high, low, high], axis=1), inverse_f_ref[...])
            for j in range(2):
                out_ref[:, r + j] = times[j * params : (j + 1) * params].reshape(blocks, part_params, steps)


def local(col_count, row_count, kernel, history, noise_weight, prior_weight):
    sensors, params, steps = kernel.shape
    part_params, vectors, _ = history.shape
    pad = -sensors % 128
    if pad:
        kernel = jnp.pad(kernel, ((0, pad), (0, 0), (0, 0)))
        noise_weight = jnp.pad(noise_weight, ((0, pad), (0, 0)))
        sensors += pad

    table = transform_table(steps)
    th, tl = split_host(table)
    ih, il = split_host(table / steps)
    table_k = jnp.asarray(np.concatenate([th, th, tl], axis=1))
    inverse_t = jnp.asarray(np.concatenate([ih.T, ih.T, il.T], axis=1))
    inverse_f = jnp.asarray(np.concatenate([ih, ih, il], axis=0))

    whole = lambda *shape: pl.BlockSpec(shape, lambda i: (0,) * len(shape))
    params_of = pltpu.CompilerParams(vmem_limit_bytes=VMEM_LIMIT)

    moved = history.transpose(1, 0, 2)
    gathered = lax.all_gather(moved, "row", axis=0)

    khat = pl.pallas_call(
        kernel_transform,
        grid=(sensors // SENSOR_BLOCK,),
        in_specs=[
            whole(2 * steps, 3 * steps),
            pl.BlockSpec((SENSOR_BLOCK, params, steps), lambda i: (i, 0, 0)),
        ],
        out_specs=pl.BlockSpec((steps, 2, SENSOR_BLOCK, 2 * params), lambda i: (0, 0, i, 0)),
        out_shape=jax.ShapeDtypeStruct((steps, 2, sensors, 2 * params), bf16),
        scratch_shapes=[pltpu.VMEM((steps * SENSOR_BLOCK, params), f32)] * 2,
        compiler_params=params_of,
        cost_estimate=pl.CostEstimate(
            flops=12 * sensors * params * steps * steps,
            bytes_accessed=12 * sensors * params * steps,
            transcendentals=0,
        ),
        name="kernel_transform",
    )(table_k, kernel)

    bits = col_count.bit_length() - 1
    total = vectors * steps
    lengths = [total // 2]
    for level in range(bits - 1):
        lengths += [total >> (level + 3)] * 2
    half_steps = steps // FREQ_BLOCK
    grad = pl.pallas_call(
        functools.partial(normal_operator, bits),
        grid=(2 * half_steps,),
        in_specs=[
            whole(2 * steps, 3 * steps),
            whole(steps, 6 * steps),
            whole(6 * steps, steps),
            whole(row_count, vectors, part_params, steps),
            whole(steps, sensors),
            pl.BlockSpec((FREQ_BLOCK, 2, sensors, 2 * params), lambda i: (lax.rem(i, half_steps), 0, 0, 0)),
        ],
        out_specs=whole(row_count, vectors, part_params, steps),
        out_shape=jax.ShapeDtypeStruct((row_count, vectors, part_params, steps), f32),
        scratch_shapes=[
            pltpu.VMEM((steps * vectors, params), f32),
            pltpu.VMEM((steps * vectors, params), f32),
            pltpu.VMEM((steps * 2 * vectors, sensors), f32),
            pltpu.VMEM((steps * 2 * vectors, params), f32),
            pltpu.VMEM((total, sensors), f32),
            pltpu.VMEM((total, sensors), f32),
            *[pltpu.VMEM((length, sensors), f32) for length in lengths],
            pltpu.SemaphoreType.DMA((2 * len(lengths),)),
            pltpu.SemaphoreType.DMA((2 * len(lengths),)),
        ],
        compiler_params=pltpu.CompilerParams(
            vmem_limit_bytes=VMEM_LIMIT, collective_id=0, has_side_effects=True
        ),
        cost_estimate=pl.CostEstimate(
            flops=32 * vectors * sensors * params * steps,
            bytes_accessed=16 * sensors * params * steps,
            transcendentals=0,
        ),
        name="normal_operator",
    )(table_k, inverse_t, inverse_f, gathered, noise_weight.T, khat)

    gradient = lax.psum_scatter(grad, "row", scatter_dimension=0, tiled=False)
    return gradient.transpose(1, 0, 2) + prior_weight[:, None, None] * history


def solution(mesh):
    in_specs = (
        P("row", "col", None),
        P(("col", "row"), None, None),
        P("row", None),
        P(("col", "row")),
    )
    out_specs = P(("col", "row"), None, None)
    return jax.shard_map(
        functools.partial(local, mesh.shape["col"], mesh.shape["row"]),
        mesh=mesh,
        in_specs=in_specs,
        out_specs=out_specs,
        check_vma=False,
    )
```

```python
import functools
import math

import jax
import jax.numpy as jnp
import ml_dtypes
import numpy as np
from jax import lax
from jax.experimental import pallas as pl
from jax.experimental.pallas import tpu as pltpu
from jax.sharding import PartitionSpec as P

f32 = jnp.float32
bf16 = jnp.bfloat16
VMEM_LIMIT = 48 * 1024 * 1024
SENSOR_BLOCK = 16
FREQ_BLOCK = 16


def transform_table(steps):
    freqs = np.arange(steps, dtype=np.int64)[:, None]
    times = np.arange(steps, dtype=np.int64)[None, :]
    phase = ((2 * freqs + 1) * times % (4 * steps)).astype(np.float64) * (math.pi / (2 * steps))
    return np.concatenate([np.cos(phase), -np.sin(phase)], axis=0)


def split_host(table):
    table = table.astype(np.float32)
    high = table.astype(ml_dtypes.bfloat16)
    low = (table - high.astype(np.float32)).astype(ml_dtypes.bfloat16)
    return high, low


def split(value):
    high = value.astype(bf16)
    return high, (value - high.astype(f32)).astype(bf16)


def matmul(lhs, rhs):
    return lax.dot_general(lhs, rhs, (((1,), (0,)), ((), ())), preferred_element_type=f32)


def matmul_nt(lhs, rhs):
    return lax.dot_general(lhs, rhs, (((1,), (1,)), ((), ())), preferred_element_type=f32)


MESH = pl.DeviceIdType.MESH
CHUNKS = 2


def greet_row(me, last, others=0):
    barrier = pltpu.get_barrier_semaphore()

    @pl.when(me > 0)
    def _():
        pl.semaphore_signal(barrier, inc=1, device_id={"row": me - 1}, device_id_type=MESH)

    @pl.when(me < last)
    def _():
        pl.semaphore_signal(barrier, inc=1, device_id={"row": me + 1}, device_id_type=MESH)

    inside = (me > 0) & (me < last)

    @pl.when(inside)
    def _():
        pl.semaphore_wait(barrier, others + 2)

    @pl.when(jnp.logical_not(inside))
    def _():
        pl.semaphore_wait(barrier, others + 1)


def kernel_transform(
    row_count, table_ref, kernel_ref, hist_ref, out_ref, all_ref, real_ref, imag_ref, own_sem, right_sems, left_sems
):
    sensors, params, steps = kernel_ref.shape
    grid_step = pl.program_id(0)
    grid_steps = pl.num_programs(0)
    me = lax.axis_index("row")
    last = row_count - 1
    half = hist_ref.shape[0] // CHUNKS
    own = pltpu.make_async_copy(hist_ref, all_ref.at[me], own_sem)

    def hop(h, c, right):
        shard = me - h if right else me + h
        sems = right_sems if right else left_sems
        rows = pl.ds(c * half, half)
        slot = all_ref.at[shard, rows]
        return pltpu.make_async_remote_copy(
            src_ref=hist_ref.at[rows] if h == 0 else slot,
            dst_ref=slot,
            send_sem=sems.at[0, h * CHUNKS + c],
            recv_sem=sems.at[1, h * CHUNKS + c],
            device_id={"row": me + 1 if right else me - 1},
            device_id_type=MESH,
        )

    def sends(h, right):
        return (me < last) & (me >= h) if right else (me > 0) & (me <= last - h)

    def receives(h, right):
        return me >= h + 1 if right else me <= last - h - 1

    def arrival(h, c, right):
        rows = pl.ds(c * half, half)
        slot = all_ref.at[me - 1 - h if right else me + 1 + h, rows]
        sems = right_sems if right else left_sems
        return pltpu.make_async_remote_copy(
            src_ref=slot,
            dst_ref=slot,
            send_sem=sems.at[0, h * CHUNKS + c],
            recv_sem=sems.at[1, h * CHUNKS + c],
            device_id={"row": me - 1 if right else me + 1},
            device_id_type=MESH,
        )

    def wait_arrival(h, c):
        for right in (True, False):

            @pl.when(receives(h, right))
            def _():
                arrival(h, c, right).wait_recv()

    def start_hop(h, c):
        for right in (True, False):

            @pl.when(sends(h, right))
            def _():
                hop(h, c, right).start()

    @pl.when(grid_step == 0)
    def _():
        greet_row(me, last)
        for c in range(CHUNKS):
            start_hop(0, c)
        own.start()

    for m in range(CHUNKS * (row_count - 2)):
        h, c = m // CHUNKS, m % CHUNKS
        due = jnp.minimum((m + 1) * grid_steps // (CHUNKS * last) + 1, grid_steps - 1)

        @pl.when(grid_step == due)
        def _():
            wait_arrival(h, c)
            start_hop(h + 1, c)

    for s in range(0, sensors, 2):
        high, low = split(kernel_ref[s : s + 2].reshape(2 * params, steps))
        spec = matmul_nt(table_ref[...], jnp.concatenate([high, low, high], axis=1))
        for j in range(2):
            cols = slice(j * params, (j + 1) * params)
            real_ref[pl.ds(s + j, steps, stride=sensors), :] = spec[:steps, cols]
            imag_ref[pl.ds(s + j, steps, stride=sensors), :] = spec[steps:, cols]

    group = 8

    def emit(i, carry):
        rows = pl.ds(pl.multiple_of(i * group * sensors, group * sensors), group * sensors)
        freqs = pl.ds(i * group, group)
        for part, ref in enumerate((real_ref, imag_ref)):
            high, low = split(ref[rows, :].reshape(group, sensors, params))
            out_ref[freqs, 0, :, part * params : (part + 1) * params] = high
            out_ref[freqs, 1, :, part * params : (part + 1) * params] = low
        return carry

    lax.fori_loop(0, steps // group, emit, 0)

    @pl.when(grid_step == grid_steps - 1)
    def _():
        own.wait()
        for c in range(CHUNKS):
            wait_arrival(row_count - 2, c)
        for h in range(row_count - 1):
            for c in range(CHUNKS):
                for right in (True, False):

                    @pl.when(sends(h, right))
                    def _():
                        hop(h, c, right).wait_send()


def col_steps(bits):
    rest = list(range(1, bits))
    return [rest, rest[::-1]]


def normal_operator(
    bits,
    table_k_ref,
    inverse_t_ref,
    inverse_f_ref,
    hist_ref,
    noise_ref,
    khat_ref,
    out_ref,
    hreal_ref,
    himag_ref,
    spec_ref,
    grad_ref,
    time_ref,
    weighted_ref,
    partial_ref,
    from_left_ref,
    from_right_ref,
    *comm,
):
    recv_refs, (send_sem, recv_sem, right_sems, left_sems) = comm[:-4], comm[-4:]
    step = pl.program_id(0)
    half_steps = pl.num_programs(0) // 2
    blocks, vectors, part_params, steps = hist_ref.shape
    params = blocks * part_params
    freq_block, _, sensors, _ = khat_ref.shape
    total = vectors * steps
    me = lax.axis_index("col")
    bit_of = [lax.rem(me // 2**b, 2) for b in range(bits)]
    partner = [me + (1 - 2 * bit_of[b]) * 2**b for b in range(bits)]
    orders = col_steps(bits)

    @pl.when(step == 0)
    def _():
        barrier = pltpu.get_barrier_semaphore()
        for b in range(bits):
            pl.semaphore_signal(barrier, inc=1, device_id={"col": partner[b]}, device_id_type=MESH)
        greet_row(lax.axis_index("row"), blocks - 1, bits)

        for r in range(0, vectors, 2):
            hist = jnp.concatenate([hist_ref[:, r + j].reshape(params, steps) for j in range(2)], axis=0)
            high, low = split(hist)
            spec = matmul_nt(table_k_ref[...], jnp.concatenate([high, low, high], axis=1))
            for j in range(2):
                cols = slice(j * params, (j + 1) * params)
                hreal_ref[pl.ds(r + j, steps, stride=vectors), :] = spec[:steps, cols]
                himag_ref[pl.ds(r + j, steps, stride=vectors), :] = spec[steps:, cols]

    @pl.when(step < half_steps)
    def _():
        for i in range(freq_block):
            f = step * freq_block + i
            rows = pl.ds(pl.multiple_of(f * vectors, vectors), vectors)
            real, imag = hreal_ref[rows, :], himag_ref[rows, :]
            both = jnp.concatenate(
                [jnp.concatenate([real, -imag], axis=1), jnp.concatenate([imag, real], axis=1)], axis=0
            )
            lhs = jnp.concatenate(split(both), axis=0)
            res = matmul_nt(lhs, khat_ref[i].reshape(2 * sensors, 2 * params))
            top, bottom = res[: 2 * vectors], res[2 * vectors :]
            spec_ref[pl.ds(pl.multiple_of(f * 2 * vectors, 2 * vectors), 2 * vectors), :] = (
                top[:, :sensors] + (top[:, sensors:] + bottom[:, :sensors])
            )

    def to_time(r):
        spec = jnp.concatenate(
            [
                jnp.concatenate(
                    [spec_ref[pl.ds(part * vectors + r + j, steps, stride=2 * vectors), :] for j in range(2)],
                    axis=1,
                )
                for part in range(2)
            ],
            axis=0,
        )
        high, low = split(spec)
        times = matmul(inverse_t_ref[...], jnp.concatenate([high, low, high], axis=0))
        for j in range(2):
            rows = pl.ds(pl.multiple_of((r + j) * steps, steps), steps)
            time_ref[rows, :] = times[:, j * sensors : (j + 1) * sensors]

    def to_spectrum(r):
        rows = [pl.ds(pl.multiple_of((r + j) * steps, steps), steps) for j in range(2)]
        high, low = split(jnp.concatenate([weighted_ref[rows[j], :] for j in range(2)], axis=1))
        spec = matmul(table_k_ref[...], jnp.concatenate([high, low, high], axis=0))
        for j in range(2):
            cols = slice(j * sensors, (j + 1) * sensors)
            spec_ref[pl.ds(r + j, steps, stride=2 * vectors), :] = spec[:steps, cols]
            spec_ref[pl.ds(vectors + r + j, steps, stride=2 * vectors), :] = spec[steps:, cols]

    @pl.when(step == half_steps - 1)
    def _():
        def rows_of(offset, length):
            return pl.ds(pl.multiple_of(offset, 8), length)

        def exchange(src, dst, sem, bit):
            copy = pltpu.make_async_remote_copy(
                src_ref=src,
                dst_ref=dst,
                send_sem=send_sem.at[sem],
                recv_sem=recv_sem.at[sem],
                device_id={"col": partner[bit]},
                device_id_type=MESH,
            )
            copy.start()
            return copy

        half = vectors // 2
        keep, give = bit_of[0] * half, (1 - bit_of[0]) * half

        def give_body(j, carry):
            to_time(give + 2 * j)
            return carry

        def keep_body(j, carry):
            to_time(keep + 2 * j)
            return carry

        lax.fori_loop(0, half // 2, give_body, 0)
        length = total // 2
        first = exchange(time_ref.at[rows_of(give * steps, length)], recv_refs[0], 0, 0)
        lax.fori_loop(0, half // 2, keep_body, 0)
        first.wait()

        length //= 2
        offsets = [keep * steps, keep * steps + length]
        for part in range(2):
            rows = rows_of(offsets[part], length)
            time_ref[rows, :] += recv_refs[0][part * length : (part + 1) * length, :]
        sem = 1
        for level in range(bits - 1):
            length //= 2
            copies = []
            for part in range(2):
                bit = orders[part][level]
                send_at = offsets[part] + (1 - bit_of[bit]) * length
                offsets[part] = offsets[part] + bit_of[bit] * length
                copies.append(exchange(time_ref.at[rows_of(send_at, length)], recv_refs[sem], sem, bit))
                sem += 1
            for part in range(2):
                copies[part].wait()
                rows = rows_of(offsets[part], length)
                time_ref[rows, :] += recv_refs[sem - 2 + part][...]

        piece = min(length, steps)
        for part in range(2):
            for j in range(length // piece):
                at = offsets[part] + j * piece
                noise = noise_ref[rows_of(lax.rem(at, steps), piece), :]
                weighted_ref[rows_of(at, piece), :] = time_ref[rows_of(at, piece), :] * noise

        for level in reversed(range(bits - 1)):
            copies = []
            for part in range(2):
                bit = orders[part][level]
                rows = weighted_ref.at[rows_of(offsets[part], length)]
                copies.append(exchange(rows, rows, sem, bit))
                sem += 1
            for part in range(2):
                copies[part].wait()
                offsets[part] = offsets[part] - bit_of[orders[part][level]] * length
            length *= 2
        rows = weighted_ref.at[rows_of(keep * steps, 2 * length)]
        last = exchange(rows, rows, sem, 0)

        def keep_spectrum(j, carry):
            to_spectrum(keep + 2 * j)
            return carry

        def give_spectrum(j, carry):
            to_spectrum(give + 2 * j)
            return carry

        lax.fori_loop(0, half // 2, keep_spectrum, 0)
        last.wait()
        lax.fori_loop(0, half // 2, give_spectrum, 0)

    @pl.when(step >= half_steps)
    def _():
        for i in range(freq_block):
            f = (step - half_steps) * freq_block + i
            base = pl.multiple_of(f * 2 * vectors, 2 * vectors)
            high, low = split(spec_ref[pl.ds(base, 2 * vectors), :])
            lhs = jnp.concatenate(
                [jnp.concatenate([high, high], axis=1), jnp.concatenate([low, jnp.zeros_like(low)], axis=1)], axis=0
            )
            res = matmul(lhs, khat_ref[i].reshape(2 * sensors, 2 * params))
            res = res[: 2 * vectors] + res[2 * vectors :]
            grad_ref[pl.ds(base, vectors), :] = res[:vectors, :params] + res[vectors:, params:]
            grad_ref[pl.ds(base + vectors, vectors), :] = res[vectors:, :params] - res[:vectors, params:]

    @pl.when(step == 2 * half_steps - 1)
    def _():
        chunk = vectors // CHUNKS
        last = blocks - 1
        row = lax.axis_index("row")

        def to_gradient(r):
            spec = jnp.concatenate(
                [
                    jnp.concatenate(
                        [grad_ref[pl.ds(part * vectors + r + j, steps, stride=2 * vectors), :] for part in range(2)],
                        axis=0,
                    ).T
                    for j in range(2)
                ],
                axis=0,
            )
            high, low = split(spec)
            times = matmul(jnp.concatenate([high, low, high], axis=1), inverse_f_ref[...])
            for j in range(2):
                partial_ref[:, r + j] = times[j * params : (j + 1) * params].reshape(blocks, part_params, steps)

        def turn(q, c, right, arriving=False):
            rows = pl.ds(c * chunk, chunk)
            sems = right_sems if right else left_sems
            landing = from_left_ref if right else from_right_ref
            return pltpu.make_async_remote_copy(
                src_ref=partial_ref.at[last - q if right else q, rows],
                dst_ref=landing.at[q, rows],
                send_sem=sems.at[0, q * CHUNKS + c],
                recv_sem=sems.at[1, q * CHUNKS + c],
                device_id={"row": row + 1 if right != arriving else row - 1},
                device_id_type=MESH,
            )

        def step_of_line(t, c):
            rows = pl.ds(c * chunk, chunk)
            for right in (True, False):
                behind = row if right else last - row
                q = t - behind
                landing = from_left_ref if right else from_right_ref

                @pl.when((q >= 0) & (q <= last - behind) & (behind > 0))
                def _():
                    turn(q, c, right, arriving=True).wait_recv()
                    shard = last - q if right else q
                    partial_ref[shard, rows] += landing[q, rows]

                @pl.when((q >= 0) & (q < last - behind))
                def _():
                    @pl.when(q >= 1)
                    def _():
                        turn(q - 1, c, right).wait_send()

                    turn(q, c, right).start()

        for c in range(CHUNKS):

            def gradient_body(j, carry):
                to_gradient(c * chunk + 2 * j)
                return carry

            lax.fori_loop(0, chunk // 2, gradient_body, 0)
            step_of_line(0, c)

        def line_body(t, carry):
            for c in range(CHUNKS):
                step_of_line(t, c)
            return carry

        lax.fori_loop(1, blocks, line_body, 0)
        out_ref[...] = partial_ref[row]

        for right in (True, False):
            behind = row if right else last - row

            @pl.when(behind < last)
            def _():
                for c in range(CHUNKS):
                    turn(last - behind - 1, c, right).wait_send()


def local(col_count, row_count, kernel, history, noise_weight, prior_weight):
    sensors, params, steps = kernel.shape
    part_params, vectors, _ = history.shape
    pad = -sensors % 128
    if pad:
        kernel = jnp.pad(kernel, ((0, pad), (0, 0), (0, 0)))
        noise_weight = jnp.pad(noise_weight, ((0, pad), (0, 0)))
        sensors += pad

    table = transform_table(steps)
    th, tl = split_host(table)
    ih, il = split_host(table / steps)
    table_k = jnp.asarray(np.concatenate([th, th, tl], axis=1))
    inverse_t = jnp.asarray(np.concatenate([ih.T, ih.T, il.T], axis=1))
    inverse_f = jnp.asarray(np.concatenate([ih, ih, il], axis=0))

    whole = lambda *shape: pl.BlockSpec(shape, lambda i: (0,) * len(shape))

    moved = history.transpose(1, 0, 2)
    hops = CHUNKS * (row_count - 1)
    anywhere = pl.BlockSpec(memory_space=pl.ANY)
    khat, gathered = pl.pallas_call(
        functools.partial(kernel_transform, row_count),
        grid=(sensors // SENSOR_BLOCK,),
        in_specs=[
            whole(2 * steps, 3 * steps),
            pl.BlockSpec((SENSOR_BLOCK, params, steps), lambda i: (i, 0, 0)),
            anywhere,
        ],
        out_specs=[
            pl.BlockSpec((steps, 2, SENSOR_BLOCK, 2 * params), lambda i: (0, 0, i, 0)),
            anywhere,
        ],
        out_shape=[
            jax.ShapeDtypeStruct((steps, 2, sensors, 2 * params), bf16),
            jax.ShapeDtypeStruct((row_count, vectors, part_params, steps), f32),
        ],
        scratch_shapes=[
            pltpu.VMEM((steps * SENSOR_BLOCK, params), f32),
            pltpu.VMEM((steps * SENSOR_BLOCK, params), f32),
            pltpu.SemaphoreType.DMA,
            pltpu.SemaphoreType.DMA((2, hops)),
            pltpu.SemaphoreType.DMA((2, hops)),
        ],
        compiler_params=pltpu.CompilerParams(
            vmem_limit_bytes=VMEM_LIMIT, collective_id=1, has_side_effects=True
        ),
        cost_estimate=pl.CostEstimate(
            flops=12 * sensors * params * steps * steps,
            bytes_accessed=12 * sensors * params * steps,
            transcendentals=0,
        ),
        name="kernel_transform",
    )(table_k, kernel, moved)

    bits = col_count.bit_length() - 1
    total = vectors * steps
    lengths = [total // 2]
    for level in range(bits - 1):
        lengths += [total >> (level + 3)] * 2
    half_steps = steps // FREQ_BLOCK
    gradient = pl.pallas_call(
        functools.partial(normal_operator, bits),
        grid=(2 * half_steps,),
        in_specs=[
            whole(2 * steps, 3 * steps),
            whole(steps, 6 * steps),
            whole(6 * steps, steps),
            whole(row_count, vectors, part_params, steps),
            whole(steps, sensors),
            pl.BlockSpec((FREQ_BLOCK, 2, sensors, 2 * params), lambda i: (lax.rem(i, half_steps), 0, 0, 0)),
        ],
        out_specs=whole(vectors, part_params, steps),
        out_shape=jax.ShapeDtypeStruct((vectors, part_params, steps), f32),
        scratch_shapes=[
            pltpu.VMEM((steps * vectors, params), f32),
            pltpu.VMEM((steps * vectors, params), f32),
            pltpu.VMEM((steps * 2 * vectors, sensors), f32),
            pltpu.VMEM((steps * 2 * vectors, params), f32),
            pltpu.VMEM((total, sensors), f32),
            pltpu.VMEM((total, sensors), f32),
            pltpu.VMEM((row_count, vectors, part_params, steps), f32),
            pltpu.VMEM((row_count - 1, vectors, part_params, steps), f32),
            pltpu.VMEM((row_count - 1, vectors, part_params, steps), f32),
            *[pltpu.VMEM((length, sensors), f32) for length in lengths],
            pltpu.SemaphoreType.DMA((2 * len(lengths),)),
            pltpu.SemaphoreType.DMA((2 * len(lengths),)),
            pltpu.SemaphoreType.DMA((2, hops)),
            pltpu.SemaphoreType.DMA((2, hops)),
        ],
        compiler_params=pltpu.CompilerParams(
            vmem_limit_bytes=VMEM_LIMIT, collective_id=0, has_side_effects=True
        ),
        cost_estimate=pl.CostEstimate(
            flops=32 * vectors * sensors * params * steps,
            bytes_accessed=16 * sensors * params * steps,
            transcendentals=0,
        ),
        name="normal_operator",
    )(table_k, inverse_t, inverse_f, gathered, noise_weight.T, khat)

    return gradient.transpose(1, 0, 2) + prior_weight[:, None, None] * history


def solution(mesh):
    in_specs = (
        P("row", "col", None),
        P(("col", "row"), None, None),
        P("row", None),
        P(("col", "row")),
    )
    out_specs = P(("col", "row"), None, None)
    return jax.shard_map(
        functools.partial(local, mesh.shape["col"], mesh.shape["row"]),
        mesh=mesh,
        in_specs=in_specs,
        out_specs=out_specs,
        check_vma=False,
    )
```

```python
import functools
import math

import jax
import jax.numpy as jnp
import ml_dtypes
import numpy as np
from jax import lax
from jax.experimental import pallas as pl
from jax.experimental.pallas import tpu as pltpu
from jax.sharding import PartitionSpec as P

f32 = jnp.float32
bf16 = jnp.bfloat16
VMEM_LIMIT = 60 * 1024 * 1024
SENSOR_BLOCK = 16
FREQ_BLOCK = 32


def transform_table(steps):
    freqs = np.arange(steps, dtype=np.int64)[:, None]
    times = np.arange(steps, dtype=np.int64)[None, :]
    phase = ((2 * freqs + 1) * times % (4 * steps)).astype(np.float64) * (math.pi / (2 * steps))
    return np.concatenate([np.cos(phase), -np.sin(phase)], axis=0)


def split_host(table):
    table = table.astype(np.float32)
    high = table.astype(ml_dtypes.bfloat16)
    low = (table - high.astype(np.float32)).astype(ml_dtypes.bfloat16)
    return high, low


def split(value):
    high = value.astype(bf16)
    return high, (value - high.astype(f32)).astype(bf16)


def matmul(lhs, rhs):
    return lax.dot_general(lhs, rhs, (((1,), (0,)), ((), ())), preferred_element_type=f32)


def matmul_nt(lhs, rhs):
    return lax.dot_general(lhs, rhs, (((1,), (1,)), ((), ())), preferred_element_type=f32)


MESH = pl.DeviceIdType.MESH
CHUNKS = 2


def greet_row(me, last, others=0):
    barrier = pltpu.get_barrier_semaphore()

    @pl.when(me > 0)
    def _():
        pl.semaphore_signal(barrier, inc=1, device_id={"row": me - 1}, device_id_type=MESH)

    @pl.when(me < last)
    def _():
        pl.semaphore_signal(barrier, inc=1, device_id={"row": me + 1}, device_id_type=MESH)

    inside = (me > 0) & (me < last)

    @pl.when(inside)
    def _():
        pl.semaphore_wait(barrier, others + 2)

    @pl.when(jnp.logical_not(inside))
    def _():
        pl.semaphore_wait(barrier, others + 1)


def kernel_transform(
    row_count, table_ref, kernel_ref, hist_ref, out_ref, all_ref, real_ref, imag_ref, own_sem, right_sems, left_sems
):
    sensors, params, steps = kernel_ref.shape
    grid_step = pl.program_id(0)
    grid_steps = pl.num_programs(0)
    me = lax.axis_index("row")
    last = row_count - 1
    half = hist_ref.shape[0] // CHUNKS
    own = pltpu.make_async_copy(hist_ref, all_ref.at[me], own_sem)

    def hop(h, c, right):
        shard = me - h if right else me + h
        sems = right_sems if right else left_sems
        rows = pl.ds(c * half, half)
        slot = all_ref.at[shard, rows]
        return pltpu.make_async_remote_copy(
            src_ref=hist_ref.at[rows] if h == 0 else slot,
            dst_ref=slot,
            send_sem=sems.at[0, h * CHUNKS + c],
            recv_sem=sems.at[1, h * CHUNKS + c],
            device_id={"row": me + 1 if right else me - 1},
            device_id_type=MESH,
        )

    def sends(h, right):
        return (me < last) & (me >= h) if right else (me > 0) & (me <= last - h)

    def receives(h, right):
        return me >= h + 1 if right else me <= last - h - 1

    def arrival(h, c, right):
        rows = pl.ds(c * half, half)
        slot = all_ref.at[me - 1 - h if right else me + 1 + h, rows]
        sems = right_sems if right else left_sems
        return pltpu.make_async_remote_copy(
            src_ref=slot,
            dst_ref=slot,
            send_sem=sems.at[0, h * CHUNKS + c],
            recv_sem=sems.at[1, h * CHUNKS + c],
            device_id={"row": me - 1 if right else me + 1},
            device_id_type=MESH,
        )

    def wait_arrival(h, c):
        for right in (True, False):

            @pl.when(receives(h, right))
            def _():
                arrival(h, c, right).wait_recv()

    def start_hop(h, c):
        for right in (True, False):

            @pl.when(sends(h, right))
            def _():
                hop(h, c, right).start()

    @pl.when(grid_step == 0)
    def _():
        greet_row(me, last)
        for c in range(CHUNKS):
            start_hop(0, c)
        own.start()

    for m in range(CHUNKS * (row_count - 2)):
        h, c = m // CHUNKS, m % CHUNKS
        due = jnp.minimum((m + 1) * grid_steps // (CHUNKS * last) + 1, grid_steps - 1)

        @pl.when(grid_step == due)
        def _():
            wait_arrival(h, c)
            start_hop(h + 1, c)

    for s in range(0, sensors, 2):
        high, low = split(kernel_ref[s : s + 2].reshape(2 * params, steps))
        spec = matmul_nt(table_ref[...], jnp.concatenate([high, low, high], axis=1))
        for j in range(2):
            cols = slice(j * params, (j + 1) * params)
            real_ref[pl.ds(s + j, steps, stride=sensors), :] = spec[:steps, cols]
            imag_ref[pl.ds(s + j, steps, stride=sensors), :] = spec[steps:, cols]

    group = 8

    def emit(i, carry):
        rows = pl.ds(pl.multiple_of(i * group * sensors, group * sensors), group * sensors)
        freqs = pl.ds(i * group, group)
        for part, ref in enumerate((real_ref, imag_ref)):
            high, low = split(ref[rows, :].reshape(group, sensors, params))
            out_ref[freqs, 0, 0, :, part * params : (part + 1) * params] = high
            out_ref[freqs, 0, 1, :, part * params : (part + 1) * params] = low
        return carry

    lax.fori_loop(0, steps // group, emit, 0)

    @pl.when(grid_step == grid_steps - 1)
    def _():
        own.wait()
        for c in range(CHUNKS):
            wait_arrival(row_count - 2, c)
        for h in range(row_count - 1):
            for c in range(CHUNKS):
                for right in (True, False):

                    @pl.when(sends(h, right))
                    def _():
                        hop(h, c, right).wait_send()


def col_steps(bits):
    rest = list(range(1, bits))
    return [rest, rest[::-1]]


def rows_of(offset, length):
    return pl.ds(pl.multiple_of(offset, 8), length)


class AllReduce:
    def __init__(self, bits, half_sensors, time_ref, weighted_ref, noise_ref, recv_refs, send_sem, recv_sem):
        me = lax.axis_index("col")
        self.bits, self.steps = bits, noise_ref.shape[0]
        self.time_ref, self.weighted_ref, self.noise_ref = time_ref, weighted_ref, noise_ref
        self.recv_refs, self.send_sem, self.recv_sem = recv_refs, send_sem, recv_sem
        self.bit_of = [lax.rem(me // 2**b, 2) for b in range(bits)]
        self.partner = [me + (1 - 2 * self.bit_of[b]) * 2**b for b in range(bits)]
        self.orders = col_steps(bits)
        total = time_ref.shape[0]
        self.core_length = total // 2
        self.keep = self.bit_of[0] * self.core_length
        self.give = (1 - self.bit_of[0]) * self.core_length
        length = self.core_length // 2
        self.offsets = [[self.keep, self.keep + length]]
        self.lengths = [length]
        for level in range(bits - 1):
            length //= 2
            self.lengths.append(length)
            self.offsets.append(
                [
                    self.offsets[-1][part] + self.bit_of[self.orders[part][level]] * length
                    for part in range(2)
                ]
            )

    def copy(self, src, dst, sem, bit):
        return pltpu.make_async_remote_copy(
            src_ref=src,
            dst_ref=dst,
            send_sem=self.send_sem.at[sem],
            recv_sem=self.recv_sem.at[sem],
            device_id={"col": self.partner[bit]},
            device_id_type=MESH,
        )

    def stage(self, k):
        levels = self.bits - 1
        if k == 0:
            return [self.copy(self.time_ref.at[rows_of(self.give, self.core_length)], self.recv_refs[0], 0, 0)]
        if k == 2 * levels + 1:
            rows = self.weighted_ref.at[rows_of(self.keep, self.core_length)]
            return [self.copy(rows, rows, 4 * levels + 1, 0)]
        copies = []
        for part in range(2):
            sem = 2 * k - 1 + part
            if k <= levels:
                bit = self.orders[part][k - 1]
                length = self.lengths[k]
                send_at = self.offsets[k - 1][part] + (1 - self.bit_of[bit]) * length
                copies.append(self.copy(self.time_ref.at[rows_of(send_at, length)], self.recv_refs[sem], sem, bit))
            else:
                level = 2 * levels - k
                bit = self.orders[part][level]
                rows = self.weighted_ref.at[rows_of(self.offsets[level + 1][part], self.lengths[level + 1])]
                copies.append(self.copy(rows, rows, sem, bit))
        return copies

    def start(self, k):
        for copy in self.stage(k):
            copy.start()

    def finish(self, k):
        levels = self.bits - 1
        copies = self.stage(k)
        for part in range(2):
            if part < len(copies):
                copies[part].wait()
            if k <= levels:
                length = self.lengths[k]
                rows = rows_of(self.offsets[k][part], length)
                if k == 0:
                    self.time_ref[rows, :] += self.recv_refs[0][part * length : (part + 1) * length, :]
                else:
                    self.time_ref[rows, :] += self.recv_refs[2 * k - 1 + part][...]
            if k == levels:
                piece = min(length, self.steps)
                for j in range(length // piece):
                    at = self.offsets[k][part] + j * piece
                    noise = self.noise_ref[rows_of(lax.rem(at, self.steps), piece), :]
                    self.weighted_ref[rows_of(at, piece), :] = self.time_ref[rows_of(at, piece), :] * noise


def normal_operator(
    bits,
    table_k_ref,
    inverse_t_ref,
    inverse_f_ref,
    hist_ref,
    noise_a_ref,
    noise_b_ref,
    khat_ref,
    out_ref,
    hreal_ref,
    himag_ref,
    spec_a_ref,
    spec_b_ref,
    grad_ref,
    time_a_ref,
    time_b_ref,
    weighted_a_ref,
    weighted_b_ref,
    partial_ref,
    from_left_ref,
    from_right_ref,
    *comm,
):
    sems = comm[-6:]
    right_sems, left_sems = sems[4:]
    recv_count = (len(comm) - 6) // 2
    step = pl.program_id(0)
    phase = pl.num_programs(0) // 4
    blocks, vectors, part_params, steps = hist_ref.shape
    params = blocks * part_params
    freq_block, _, _, half, _ = khat_ref.shape
    pairs = vectors // 2
    lanes = 2 * half
    spec_refs = (spec_a_ref, spec_b_ref)
    time_refs = (time_a_ref, time_b_ref)
    weighted_refs = (weighted_a_ref, weighted_b_ref)
    reduces = [
        AllReduce(
            bits, half, time_refs[h], weighted_refs[h], (noise_a_ref, noise_b_ref)[h],
            comm[h * recv_count : (h + 1) * recv_count], sems[2 * h], sems[2 * h + 1],
        )
        for h in range(2)
    ]
    stages = 2 * bits

    @pl.when(step == 0)
    def _():
        barrier = pltpu.get_barrier_semaphore()
        for b in range(bits):
            pl.semaphore_signal(barrier, inc=1, device_id={"col": reduces[0].partner[b]}, device_id_type=MESH)
        greet_row(lax.axis_index("row"), blocks - 1, bits)

        for r in range(0, vectors, 2):
            hist = jnp.concatenate([hist_ref[:, r + j].reshape(params, steps) for j in range(2)], axis=0)
            high, low = split(hist)
            spec = matmul_nt(table_k_ref[...], jnp.concatenate([high, low, high], axis=1))
            for j in range(2):
                cols = slice(j * params, (j + 1) * params)
                rows = pl.ds(j * pairs + r // 2, steps, stride=vectors)
                hreal_ref[rows, :] = spec[:steps, cols]
                himag_ref[rows, :] = spec[steps:, cols]

    def forward(h):
        for i in range(freq_block):
            f = lax.rem(step, phase) * freq_block + i
            rows = pl.ds(pl.multiple_of(f * vectors, vectors), vectors)
            real, imag = hreal_ref[rows, :], himag_ref[rows, :]
            top, bottom = jnp.concatenate([real, -imag], axis=1), jnp.concatenate([imag, real], axis=1)
            both = jnp.concatenate([top[:pairs], bottom[:pairs], top[pairs:], bottom[pairs:]], axis=0)
            lhs = jnp.concatenate(split(both), axis=0)
            res = matmul_nt(lhs, khat_ref[i, 0].reshape(lanes, 2 * params))
            high, low = res[: 2 * vectors], res[2 * vectors :]
            data = high[:, :half] + (high[:, half:] + low[:, :half])
            spec_refs[h][rows, :] = jnp.concatenate([data[:vectors], data[vectors:]], axis=1)

    def to_time(h, pair):
        spec_ref = spec_refs[h]
        spec = jnp.concatenate(
            [
                jnp.concatenate(
                    [spec_ref[pl.ds(part * pairs + pair + j, steps, stride=vectors), :] for j in range(2)],
                    axis=1,
                )
                for part in range(2)
            ],
            axis=0,
        )
        high, low = split(spec)
        times = matmul(inverse_t_ref[...], jnp.concatenate([high, low, high], axis=0))
        for j in range(2):
            time_refs[h][rows_of((pair + j) * steps, steps), :] = times[:, j * lanes : (j + 1) * lanes]

    def to_spectrum(h, pair):
        weighted = [weighted_refs[h][rows_of((pair + j) * steps, steps), :] for j in range(2)]
        high, low = split(jnp.concatenate(weighted, axis=1))
        spec = matmul(table_k_ref[...], jnp.concatenate([high, low, high], axis=0))
        for j in range(2):
            cols = slice(j * lanes, (j + 1) * lanes)
            spec_refs[h][pl.ds(pair + j, steps, stride=vectors), :] = spec[:steps, cols]
            spec_refs[h][pl.ds(pairs + pair + j, steps, stride=vectors), :] = spec[steps:, cols]

    def over_pairs(body, h, first):
        def one(j, carry):
            body(h, first + 2 * j)
            return carry

        lax.fori_loop(0, pairs // 4, one, 0)

    def begin(h):
        reduce = reduces[h]
        over_pairs(to_time, h, (1 - reduce.bit_of[0]) * (pairs // 2))
        reduce.start(0)
        over_pairs(to_time, h, reduce.bit_of[0] * (pairs // 2))

    def end(h):
        reduce = reduces[h]
        over_pairs(to_spectrum, h, reduce.bit_of[0] * (pairs // 2))
        reduce.finish(stages - 1)
        over_pairs(to_spectrum, h, (1 - reduce.bit_of[0]) * (pairs // 2))

    shares = [1.9] + [1 + 2.6 / 2**level for level in range(bits - 1)]
    shares = shares + shares[::-1]

    def events(h, base):
        done = 0.0
        for k in range(1, stages):
            done += shares[k - 1]

            @pl.when(step == base + jnp.minimum((int(1024 * done / sum(shares)) * phase + 1023) // 1024, phase - 1))
            def _():
                reduces[h].finish(k - 1)
                reduces[h].start(k)

    def backward(h):
        for i in range(freq_block):
            f = lax.rem(step, phase) * freq_block + i
            base = pl.multiple_of(f * 2 * vectors, 2 * vectors)
            mine = spec_refs[h][pl.ds(pl.multiple_of(f * vectors, vectors), vectors), :]
            swapped = jnp.concatenate([mine[:, half:], mine[:, :half]], axis=1)
            left = lax.broadcasted_iota(jnp.int32, mine.shape, 1) < half
            both = jnp.concatenate([jnp.where(left, mine, swapped), jnp.where(left, swapped, mine)], axis=0)
            high, low = split(both)
            left = lax.broadcasted_iota(jnp.int32, both.shape, 1) < half
            low = jnp.where(left, low.astype(f32), 0.0).astype(bf16)
            res = matmul(jnp.concatenate([high, low], axis=0), khat_ref[i, 0].reshape(lanes, 2 * params))
            res = res[: 2 * vectors] + res[2 * vectors :]
            real = jnp.concatenate([res[:pairs], res[vectors : vectors + pairs]], axis=0)
            imag = jnp.concatenate([res[pairs:vectors], res[vectors + pairs :]], axis=0)
            grad_real = real[:, :params] + imag[:, params:]
            grad_imag = imag[:, :params] - real[:, params:]
            if h == 0:
                grad_ref[pl.ds(base, vectors), :] = grad_real
                grad_ref[pl.ds(base + vectors, vectors), :] = grad_imag
            else:
                grad_ref[pl.ds(base, vectors), :] += grad_real
                grad_ref[pl.ds(base + vectors, vectors), :] += grad_imag

    @pl.when(step < phase)
    def _():
        forward(0)

    @pl.when(step == phase - 1)
    def _():
        begin(0)

    events(0, phase)

    @pl.when((step >= phase) & (step < 2 * phase))
    def _():
        forward(1)

    @pl.when(step == 2 * phase - 1)
    def _():
        begin(1)
        end(0)

    events(1, 2 * phase)

    @pl.when((step >= 2 * phase) & (step < 3 * phase))
    def _():
        backward(0)

    @pl.when(step == 3 * phase - 1)
    def _():
        end(1)

    @pl.when(step >= 3 * phase)
    def _():
        backward(1)

    @pl.when(step == 4 * phase - 1)
    def _():
        chunk = vectors // CHUNKS
        last = blocks - 1
        row = lax.axis_index("row")

        def to_gradient(r):
            spec = jnp.concatenate(
                [
                    jnp.concatenate(
                        [
                            grad_ref[pl.ds(part * vectors + j * pairs + r // 2, steps, stride=2 * vectors), :]
                            for part in range(2)
                        ],
                        axis=0,
                    ).T
                    for j in range(2)
                ],
                axis=0,
            )
            high, low = split(spec)
            times = matmul(jnp.concatenate([high, low, high], axis=1), inverse_f_ref[...])
            for j in range(2):
                partial_ref[:, r + j] = times[j * params : (j + 1) * params].reshape(blocks, part_params, steps)

        def turn(q, c, right, arriving=False):
            rows = pl.ds(c * chunk, chunk)
            sems = right_sems if right else left_sems
            landing = from_left_ref if right else from_right_ref
            return pltpu.make_async_remote_copy(
                src_ref=partial_ref.at[last - q if right else q, rows],
                dst_ref=landing.at[q, rows],
                send_sem=sems.at[0, q * CHUNKS + c],
                recv_sem=sems.at[1, q * CHUNKS + c],
                device_id={"row": row + 1 if right != arriving else row - 1},
                device_id_type=MESH,
            )

        def step_of_line(t, c):
            rows = pl.ds(c * chunk, chunk)
            for right in (True, False):
                behind = row if right else last - row
                q = t - behind
                landing = from_left_ref if right else from_right_ref

                @pl.when((q >= 0) & (q <= last - behind) & (behind > 0))
                def _():
                    turn(q, c, right, arriving=True).wait_recv()
                    shard = last - q if right else q
                    partial_ref[shard, rows] += landing[q, rows]

                @pl.when((q >= 0) & (q < last - behind))
                def _():
                    @pl.when(q >= 1)
                    def _():
                        turn(q - 1, c, right).wait_send()

                    turn(q, c, right).start()

        for c in range(CHUNKS):

            def gradient_body(j, carry):
                to_gradient(c * chunk + 2 * j)
                return carry

            lax.fori_loop(0, chunk // 2, gradient_body, 0)
            step_of_line(0, c)

        def line_body(t, carry):
            for c in range(CHUNKS):
                step_of_line(t, c)
            return carry

        lax.fori_loop(1, blocks, line_body, 0)
        out_ref[...] = partial_ref[row]

        for right in (True, False):
            behind = row if right else last - row

            @pl.when(behind < last)
            def _():
                for c in range(CHUNKS):
                    turn(last - behind - 1, c, right).wait_send()


def local(col_count, row_count, kernel, history, noise_weight, prior_weight):
    sensors, params, steps = kernel.shape
    part_params, vectors, _ = history.shape
    pad = -sensors % 128
    if pad:
        kernel = jnp.pad(kernel, ((0, pad), (0, 0), (0, 0)))
        noise_weight = jnp.pad(noise_weight, ((0, pad), (0, 0)))
        sensors += pad

    table = transform_table(steps)
    th, tl = split_host(table)
    ih, il = split_host(table / steps)
    table_k = jnp.asarray(np.concatenate([th, th, tl], axis=1))
    inverse_t = jnp.asarray(np.concatenate([ih.T, ih.T, il.T], axis=1))
    inverse_f = jnp.asarray(np.concatenate([ih, ih, il], axis=0))

    whole = lambda *shape: pl.BlockSpec(shape, lambda i: (0,) * len(shape))

    moved = history.transpose(1, 0, 2)
    hops = CHUNKS * (row_count - 1)
    per_half = sensors // 2 // SENSOR_BLOCK
    anywhere = pl.BlockSpec(memory_space=pl.ANY)
    khat, gathered = pl.pallas_call(
        functools.partial(kernel_transform, row_count),
        grid=(sensors // SENSOR_BLOCK,),
        in_specs=[
            whole(2 * steps, 3 * steps),
            pl.BlockSpec((SENSOR_BLOCK, params, steps), lambda i: (i, 0, 0)),
            anywhere,
        ],
        out_specs=[
            pl.BlockSpec(
                (steps, 1, 2, SENSOR_BLOCK, 2 * params), lambda i: (0, i // per_half, 0, lax.rem(i, per_half), 0)
            ),
            anywhere,
        ],
        out_shape=[
            jax.ShapeDtypeStruct((steps, 2, 2, sensors // 2, 2 * params), bf16),
            jax.ShapeDtypeStruct((row_count, vectors, part_params, steps), f32),
        ],
        scratch_shapes=[
            pltpu.VMEM((steps * SENSOR_BLOCK, params), f32),
            pltpu.VMEM((steps * SENSOR_BLOCK, params), f32),
            pltpu.SemaphoreType.DMA,
            pltpu.SemaphoreType.DMA((2, hops)),
            pltpu.SemaphoreType.DMA((2, hops)),
        ],
        compiler_params=pltpu.CompilerParams(
            vmem_limit_bytes=VMEM_LIMIT, collective_id=1, has_side_effects=True
        ),
        cost_estimate=pl.CostEstimate(
            flops=12 * sensors * params * steps * steps,
            bytes_accessed=12 * sensors * params * steps,
            transcendentals=0,
        ),
        name="kernel_transform",
    )(table_k, kernel, moved)

    bits = col_count.bit_length() - 1
    total = vectors * steps
    rows = total // 2
    lengths = [rows // 2]
    for level in range(bits - 1):
        lengths += [rows >> (level + 3)] * 2
    phase = steps // FREQ_BLOCK
    noise = noise_weight.T
    noise_halves = [jnp.tile(noise[:, h * sensors // 2 : (h + 1) * sensors // 2], (1, 2)) for h in range(2)]
    gradient = pl.pallas_call(
        functools.partial(normal_operator, bits),
        grid=(4 * phase,),
        in_specs=[
            whole(2 * steps, 3 * steps),
            whole(steps, 6 * steps),
            whole(6 * steps, steps),
            whole(row_count, vectors, part_params, steps),
            whole(steps, sensors),
            whole(steps, sensors),
            pl.BlockSpec(
                (FREQ_BLOCK, 1, 2, sensors // 2, 2 * params),
                lambda i: (lax.rem(i, phase), lax.rem(i // phase, 2), 0, 0, 0),
            ),
        ],
        out_specs=whole(vectors, part_params, steps),
        out_shape=jax.ShapeDtypeStruct((vectors, part_params, steps), f32),
        scratch_shapes=[
            pltpu.VMEM((steps * vectors, params), f32),
            pltpu.VMEM((steps * vectors, params), f32),
            pltpu.VMEM((steps * vectors, sensors), f32),
            pltpu.VMEM((steps * vectors, sensors), f32),
            pltpu.VMEM((steps * 2 * vectors, params), f32),
            *[pltpu.VMEM((rows, sensors), f32)] * 4,
            pltpu.VMEM((row_count, vectors, part_params, steps), f32),
            pltpu.VMEM((row_count - 1, vectors, part_params, steps), f32),
            pltpu.VMEM((row_count - 1, vectors, part_params, steps), f32),
            *[pltpu.VMEM((length, sensors), f32) for length in lengths] * 2,
            *[pltpu.SemaphoreType.DMA((2 * len(lengths),))] * 4,
            pltpu.SemaphoreType.DMA((2, hops)),
            pltpu.SemaphoreType.DMA((2, hops)),
        ],
        compiler_params=pltpu.CompilerParams(
            vmem_limit_bytes=VMEM_LIMIT, collective_id=0, has_side_effects=True
        ),
        cost_estimate=pl.CostEstimate(
            flops=32 * vectors * sensors * params * steps,
            bytes_accessed=16 * sensors * params * steps,
            transcendentals=0,
        ),
        name="normal_operator",
    )(table_k, inverse_t, inverse_f, gathered, *noise_halves, khat)

    return gradient.transpose(1, 0, 2) + prior_weight[:, None, None] * history


def solution(mesh):
    in_specs = (
        P("row", "col", None),
        P(("col", "row"), None, None),
        P("row", None),
        P(("col", "row")),
    )
    out_specs = P(("col", "row"), None, None)
    return jax.shard_map(
        functools.partial(local, mesh.shape["col"], mesh.shape["row"]),
        mesh=mesh,
        in_specs=in_specs,
        out_specs=out_specs,
        check_vma=False,
    )
```

```python
import functools
import math

import jax
import jax.numpy as jnp
import ml_dtypes
import numpy as np
from jax import lax
from jax.experimental import pallas as pl
from jax.experimental.pallas import tpu as pltpu
from jax.sharding import PartitionSpec as P

f32 = jnp.float32
bf16 = jnp.bfloat16
VMEM_LIMIT = 60 * 1024 * 1024
SENSOR_BLOCK = 16
FREQ_BLOCK = 32
GROUP = 8


def transform_table(steps):
    freqs = np.arange(steps, dtype=np.int64)[:, None]
    times = np.arange(steps, dtype=np.int64)[None, :]
    phase = ((2 * freqs + 1) * times % (4 * steps)).astype(np.float64) * (math.pi / (2 * steps))
    return np.concatenate([np.cos(phase), -np.sin(phase)], axis=0)


def split_host(table):
    table = table.astype(np.float32)
    high = table.astype(ml_dtypes.bfloat16)
    low = (table - high.astype(np.float32)).astype(ml_dtypes.bfloat16)
    return high, low


def split(value):
    high = value.astype(bf16)
    return high, (value - high.astype(f32)).astype(bf16)


def matmul(lhs, rhs):
    return lax.dot_general(lhs, rhs, (((1,), (0,)), ((), ())), preferred_element_type=f32)


def matmul_nt(lhs, rhs):
    return lax.dot_general(lhs, rhs, (((1,), (1,)), ((), ())), preferred_element_type=f32)


MESH = pl.DeviceIdType.MESH
CHUNKS = 2


def greet_row(me, last, others=0):
    barrier = pltpu.get_barrier_semaphore()

    @pl.when(me > 0)
    def _():
        pl.semaphore_signal(barrier, inc=1, device_id={"row": me - 1}, device_id_type=MESH)

    @pl.when(me < last)
    def _():
        pl.semaphore_signal(barrier, inc=1, device_id={"row": me + 1}, device_id_type=MESH)

    inside = (me > 0) & (me < last)

    @pl.when(inside)
    def _():
        pl.semaphore_wait(barrier, others + 2)

    @pl.when(jnp.logical_not(inside))
    def _():
        pl.semaphore_wait(barrier, others + 1)


def kernel_transform(
    row_count, table_ref, kernel_ref, raw_ref, out_ref, all_ref, hist_ref, real_ref, imag_ref, *sems
):
    own_sem, right_sems, left_sems = sems
    sensors, params, steps = kernel_ref.shape
    grid_step = pl.program_id(0)
    grid_steps = pl.num_programs(0)
    me = lax.axis_index("row")
    last = row_count - 1
    half = hist_ref.shape[0] // CHUNKS
    own = pltpu.make_async_copy(hist_ref, all_ref.at[me], own_sem)

    def hop(h, c, right):
        shard = me - h if right else me + h
        sems = right_sems if right else left_sems
        rows = pl.ds(c * half, half)
        slot = all_ref.at[shard, rows]
        return pltpu.make_async_remote_copy(
            src_ref=hist_ref.at[rows] if h == 0 else slot,
            dst_ref=slot,
            send_sem=sems.at[0, h * CHUNKS + c],
            recv_sem=sems.at[1, h * CHUNKS + c],
            device_id={"row": me + 1 if right else me - 1},
            device_id_type=MESH,
        )

    def sends(h, right):
        return (me < last) & (me >= h) if right else (me > 0) & (me <= last - h)

    def receives(h, right):
        return me >= h + 1 if right else me <= last - h - 1

    def arrival(h, c, right):
        rows = pl.ds(c * half, half)
        slot = all_ref.at[me - 1 - h if right else me + 1 + h, rows]
        sems = right_sems if right else left_sems
        return pltpu.make_async_remote_copy(
            src_ref=slot,
            dst_ref=slot,
            send_sem=sems.at[0, h * CHUNKS + c],
            recv_sem=sems.at[1, h * CHUNKS + c],
            device_id={"row": me - 1 if right else me + 1},
            device_id_type=MESH,
        )

    def wait_arrival(h, c):
        for right in (True, False):

            @pl.when(receives(h, right))
            def _():
                arrival(h, c, right).wait_recv()

    def start_hop(h, c):
        for right in (True, False):

            @pl.when(sends(h, right))
            def _():
                hop(h, c, right).start()

    @pl.when(grid_step == 0)
    def _():
        hist_ref[...] = jnp.swapaxes(raw_ref[...], 0, 1)
        greet_row(me, last)
        for c in range(CHUNKS):
            start_hop(0, c)
        own.start()

    for m in range(CHUNKS * (row_count - 2)):
        h, c = m // CHUNKS, m % CHUNKS
        due = jnp.minimum((m + 1) * grid_steps // (CHUNKS * last) + 1, grid_steps - 1)

        @pl.when(grid_step == due)
        def _():
            wait_arrival(h, c)
            start_hop(h + 1, c)

    for s in range(0, sensors, 2):
        high, low = split(kernel_ref[s : s + 2].reshape(2 * params, steps))
        spec = matmul_nt(table_ref[...], jnp.concatenate([high, low, high], axis=1))
        for j in range(2):
            cols = slice(j * params, (j + 1) * params)
            real_ref[pl.ds(s + j, steps, stride=sensors), :] = spec[:steps, cols]
            imag_ref[pl.ds(s + j, steps, stride=sensors), :] = spec[steps:, cols]

    group = 8

    def emit(i, carry):
        rows = pl.ds(pl.multiple_of(i * group * sensors, group * sensors), group * sensors)
        freqs = pl.ds(i * group, group)
        for part, ref in enumerate((real_ref, imag_ref)):
            high, low = split(ref[rows, :].reshape(group, sensors, params))
            out_ref[freqs, 0, 0, :, part * params : (part + 1) * params] = high
            out_ref[freqs, 0, 1, :, part * params : (part + 1) * params] = low
        return carry

    lax.fori_loop(0, steps // group, emit, 0)

    @pl.when(grid_step == grid_steps - 1)
    def _():
        own.wait()
        for c in range(CHUNKS):
            wait_arrival(row_count - 2, c)
        for h in range(row_count - 1):
            for c in range(CHUNKS):
                for right in (True, False):

                    @pl.when(sends(h, right))
                    def _():
                        hop(h, c, right).wait_send()


def col_steps(bits):
    rest = list(range(1, bits))
    return [rest, rest[::-1]]


def rows_of(offset, length):
    return pl.ds(pl.multiple_of(offset, 8), length)


class AllReduce:
    def __init__(self, bits, sensors, time_ref, weighted_ref, noise_ref, recv_refs, send_sem, recv_sem):
        me = lax.axis_index("col")
        self.bits, self.steps, self.sensors = bits, noise_ref.shape[0], sensors
        self.time_ref, self.weighted_ref, self.noise_ref = time_ref, weighted_ref, noise_ref
        self.recv_refs, self.send_sem, self.recv_sem = recv_refs, send_sem, recv_sem
        self.bit_of = [lax.rem(me // 2**b, 2) for b in range(bits)]
        self.partner = [me + (1 - 2 * self.bit_of[b]) * 2**b for b in range(bits)]
        self.orders = col_steps(bits)
        total = time_ref.shape[0]
        self.core_length = total // 2
        self.keep = self.bit_of[0] * self.core_length
        self.give = (1 - self.bit_of[0]) * self.core_length
        length = self.core_length // 2
        self.offsets = [[self.keep, self.keep + length]]
        self.lengths = [length]
        for level in range(bits - 1):
            length //= 2
            self.lengths.append(length)
            self.offsets.append(
                [
                    self.offsets[-1][part] + self.bit_of[self.orders[part][level]] * length
                    for part in range(2)
                ]
            )

    def copy(self, src, dst, sem, bit):
        return pltpu.make_async_remote_copy(
            src_ref=src,
            dst_ref=dst,
            send_sem=self.send_sem.at[sem],
            recv_sem=self.recv_sem.at[sem],
            device_id={"col": self.partner[bit]},
            device_id_type=MESH,
        )

    def stage(self, k):
        levels = self.bits - 1
        if k == 0:
            return [self.copy(self.time_ref.at[rows_of(self.give, self.core_length)], self.recv_refs[0], 0, 0)]
        if k == 2 * levels + 1:
            rows = self.weighted_ref.at[rows_of(self.keep, self.core_length)]
            return [self.copy(rows, rows, 4 * levels + 1, 0)]
        copies = []
        for part in range(2):
            sem = 2 * k - 1 + part
            if k <= levels:
                bit = self.orders[part][k - 1]
                length = self.lengths[k]
                send_at = self.offsets[k - 1][part] + (1 - self.bit_of[bit]) * length
                copies.append(self.copy(self.time_ref.at[rows_of(send_at, length)], self.recv_refs[sem], sem, bit))
            else:
                level = 2 * levels - k
                bit = self.orders[part][level]
                rows = self.weighted_ref.at[rows_of(self.offsets[level + 1][part], self.lengths[level + 1])]
                copies.append(self.copy(rows, rows, sem, bit))
        return copies

    def start(self, k):
        for copy in self.stage(k):
            copy.start()

    def finish(self, k):
        levels = self.bits - 1
        copies = self.stage(k)
        for part in range(2):
            if part < len(copies):
                copies[part].wait()
            if k <= levels:
                length = self.lengths[k]
                rows = rows_of(self.offsets[k][part], length)
                if k == 0:
                    self.time_ref[rows, :] += self.recv_refs[0][part * length : (part + 1) * length, :]
                else:
                    self.time_ref[rows, :] += self.recv_refs[2 * k - 1 + part][...]
            if k == levels:
                piece = min(length, self.steps)
                for j in range(length // piece):
                    at = self.offsets[k][part] + j * piece
                    noise = self.noise_ref[rows_of(lax.rem(at, self.steps), piece), :][:, self.sensors]
                    noise = jnp.concatenate([noise, noise], axis=1)
                    self.weighted_ref[rows_of(at, piece), :] = self.time_ref[rows_of(at, piece), :] * noise


def normal_operator(
    bits,
    table_k_ref,
    inverse_t_ref,
    inverse_f_ref,
    hist_ref,
    weights_ref,
    khat_ref,
    out_ref,
    hreal_ref,
    himag_ref,
    noise_ref,
    spec_a_ref,
    spec_b_ref,
    grad_ref,
    time_a_ref,
    time_b_ref,
    weighted_a_ref,
    weighted_b_ref,
    partial_ref,
    from_left_ref,
    from_right_ref,
    *comm,
):
    sems = comm[-6:]
    right_sems, left_sems = sems[4:]
    recv_count = (len(comm) - 6) // 2
    step = pl.program_id(0)
    phase = pl.num_programs(0) // 4
    blocks, vectors, part_params, steps = hist_ref.shape
    params = blocks * part_params
    freq_block, _, _, half, _ = khat_ref.shape
    pairs = vectors // 2
    lanes = 2 * half
    spec_refs = (spec_a_ref, spec_b_ref)
    time_refs = (time_a_ref, time_b_ref)
    weighted_refs = (weighted_a_ref, weighted_b_ref)
    reduces = [
        AllReduce(
            bits, slice(h * half, (h + 1) * half), time_refs[h], weighted_refs[h], noise_ref,
            comm[h * recv_count : (h + 1) * recv_count], sems[2 * h], sems[2 * h + 1],
        )
        for h in range(2)
    ]
    stages = 2 * bits

    @pl.when(step == 0)
    def _():
        barrier = pltpu.get_barrier_semaphore()
        for b in range(bits):
            pl.semaphore_signal(barrier, inc=1, device_id={"col": reduces[0].partner[b]}, device_id_type=MESH)
        greet_row(lax.axis_index("row"), blocks - 1, bits)

        noise_ref[...] = weights_ref[...].T
        for r in range(0, vectors, 2):
            hist = jnp.concatenate([hist_ref[:, r + j].reshape(params, steps) for j in range(2)], axis=0)
            high, low = split(hist)
            spec = matmul_nt(table_k_ref[...], jnp.concatenate([high, low, high], axis=1))
            for j in range(2):
                cols = slice(j * params, (j + 1) * params)
                rows = pl.ds(j * pairs + r // 2, steps, stride=vectors)
                hreal_ref[rows, :] = spec[:steps, cols]
                himag_ref[rows, :] = spec[steps:, cols]

    def grouped(product):
        for first in range(0, freq_block, GROUP):
            stores = [product(first + i) for i in range(GROUP)]
            for ref, rows, value in sum(stores, []):
                ref[rows, :] = value

    def forward(h):
        def product(i):
            f = lax.rem(step, phase) * freq_block + i
            rows = pl.ds(pl.multiple_of(f * vectors, vectors), vectors)
            real, imag = hreal_ref[rows, :], himag_ref[rows, :]
            top, bottom = jnp.concatenate([real, -imag], axis=1), jnp.concatenate([imag, real], axis=1)
            both = jnp.concatenate([top[:pairs], bottom[:pairs], top[pairs:], bottom[pairs:]], axis=0)
            lhs = jnp.concatenate(split(both), axis=0)
            res = matmul_nt(lhs, khat_ref[i, 0].reshape(lanes, 2 * params))
            high, low = res[: 2 * vectors], res[2 * vectors :]
            data = high[:, :half] + (high[:, half:] + low[:, :half])
            return [(spec_refs[h], rows, jnp.concatenate([data[:vectors], data[vectors:]], axis=1))]

        grouped(product)

    def to_time(h, pair):
        spec_ref = spec_refs[h]
        spec = jnp.concatenate(
            [
                jnp.concatenate(
                    [spec_ref[pl.ds(part * pairs + pair + j, steps, stride=vectors), :] for j in range(2)],
                    axis=1,
                )
                for part in range(2)
            ],
            axis=0,
        )
        high, low = split(spec)
        times = matmul(inverse_t_ref[...], jnp.concatenate([high, low, high], axis=0))
        for j in range(2):
            time_refs[h][rows_of((pair + j) * steps, steps), :] = times[:, j * lanes : (j + 1) * lanes]

    def to_spectrum(h, pair):
        weighted = [weighted_refs[h][rows_of((pair + j) * steps, steps), :] for j in range(2)]
        high, low = split(jnp.concatenate(weighted, axis=1))
        spec = matmul(table_k_ref[...], jnp.concatenate([high, low, high], axis=0))
        for j in range(2):
            cols = slice(j * lanes, (j + 1) * lanes)
            spec_refs[h][pl.ds(pair + j, steps, stride=vectors), :] = spec[:steps, cols]
            spec_refs[h][pl.ds(pairs + pair + j, steps, stride=vectors), :] = spec[steps:, cols]

    def over_pairs(body, h, first):
        def one(j, carry):
            body(h, first + 2 * j)
            return carry

        lax.fori_loop(0, pairs // 4, one, 0)

    def begin(h):
        reduce = reduces[h]
        over_pairs(to_time, h, (1 - reduce.bit_of[0]) * (pairs // 2))
        reduce.start(0)
        over_pairs(to_time, h, reduce.bit_of[0] * (pairs // 2))

    def end(h):
        reduce = reduces[h]
        over_pairs(to_spectrum, h, reduce.bit_of[0] * (pairs // 2))
        reduce.finish(stages - 1)
        over_pairs(to_spectrum, h, (1 - reduce.bit_of[0]) * (pairs // 2))

    shares = [1.9] + [1 + 2.6 / 2**level for level in range(bits - 1)]
    shares = shares + shares[::-1]

    def events(h, base):
        done = 0.0
        for k in range(1, stages):
            done += shares[k - 1]

            @pl.when(step == base + jnp.minimum((int(1024 * done / sum(shares)) * phase + 1023) // 1024, phase - 1))
            def _():
                reduces[h].finish(k - 1)
                reduces[h].start(k)

    def backward(h):
        def product(i):
            f = lax.rem(step, phase) * freq_block + i
            base = pl.multiple_of(f * 2 * vectors, 2 * vectors)
            mine = spec_refs[h][pl.ds(pl.multiple_of(f * vectors, vectors), vectors), :]
            swapped = jnp.concatenate([mine[:, half:], mine[:, :half]], axis=1)
            left = lax.broadcasted_iota(jnp.int32, mine.shape, 1) < half
            both = jnp.concatenate([jnp.where(left, mine, swapped), jnp.where(left, swapped, mine)], axis=0)
            high, low = split(both)
            left = lax.broadcasted_iota(jnp.int32, both.shape, 1) < half
            low = jnp.where(left, low.astype(f32), 0.0).astype(bf16)
            res = matmul(jnp.concatenate([high, low], axis=0), khat_ref[i, 0].reshape(lanes, 2 * params))
            res = res[: 2 * vectors] + res[2 * vectors :]
            real = jnp.concatenate([res[:pairs], res[vectors : vectors + pairs]], axis=0)
            imag = jnp.concatenate([res[pairs:vectors], res[vectors + pairs :]], axis=0)
            values = [real[:, :params] + imag[:, params:], imag[:, :params] - real[:, params:]]
            rows = [pl.ds(base, vectors), pl.ds(base + vectors, vectors)]
            if h == 1:
                values = [value + grad_ref[at, :] for value, at in zip(values, rows)]
            return [(grad_ref, at, value) for value, at in zip(values, rows)]

        grouped(product)

    @pl.when(step < phase)
    def _():
        forward(0)

    @pl.when(step == phase - 1)
    def _():
        begin(0)

    events(0, phase)

    @pl.when((step >= phase) & (step < 2 * phase))
    def _():
        forward(1)

    @pl.when(step == 2 * phase - 1)
    def _():
        begin(1)
        end(0)

    events(1, 2 * phase)

    @pl.when((step >= 2 * phase) & (step < 3 * phase))
    def _():
        backward(0)

    @pl.when(step == 3 * phase - 1)
    def _():
        end(1)

    @pl.when(step >= 3 * phase)
    def _():
        backward(1)

    @pl.when(step == 4 * phase - 1)
    def _():
        chunk = vectors // CHUNKS
        last = blocks - 1
        row = lax.axis_index("row")

        def to_gradient(r):
            spec = jnp.concatenate(
                [
                    jnp.concatenate(
                        [
                            grad_ref[pl.ds(part * vectors + j * pairs + r // 2, steps, stride=2 * vectors), :]
                            for part in range(2)
                        ],
                        axis=0,
                    ).T
                    for j in range(2)
                ],
                axis=0,
            )
            high, low = split(spec)
            times = matmul(jnp.concatenate([high, low, high], axis=1), inverse_f_ref[...])
            for j in range(2):
                partial_ref[:, r + j] = times[j * params : (j + 1) * params].reshape(blocks, part_params, steps)

        def turn(q, c, right, arriving=False):
            rows = pl.ds(c * chunk, chunk)
            sems = right_sems if right else left_sems
            landing = from_left_ref if right else from_right_ref
            return pltpu.make_async_remote_copy(
                src_ref=partial_ref.at[last - q if right else q, rows],
                dst_ref=landing.at[q, rows],
                send_sem=sems.at[0, q * CHUNKS + c],
                recv_sem=sems.at[1, q * CHUNKS + c],
                device_id={"row": row + 1 if right != arriving else row - 1},
                device_id_type=MESH,
            )

        def step_of_line(t, c):
            rows = pl.ds(c * chunk, chunk)
            for right in (True, False):
                behind = row if right else last - row
                q = t - behind
                landing = from_left_ref if right else from_right_ref

                @pl.when((q >= 0) & (q <= last - behind) & (behind > 0))
                def _():
                    turn(q, c, right, arriving=True).wait_recv()
                    shard = last - q if right else q
                    partial_ref[shard, rows] += landing[q, rows]

                @pl.when((q >= 0) & (q < last - behind))
                def _():
                    @pl.when(q >= 1)
                    def _():
                        turn(q - 1, c, right).wait_send()

                    turn(q, c, right).start()

        for c in range(CHUNKS):

            def gradient_body(j, carry):
                to_gradient(c * chunk + 2 * j)
                return carry

            lax.fori_loop(0, chunk // 2, gradient_body, 0)
            step_of_line(0, c)

        def line_body(t, carry):
            for c in range(CHUNKS):
                step_of_line(t, c)
            return carry

        lax.fori_loop(1, blocks, line_body, 0)
        out_ref[...] = jnp.swapaxes(partial_ref[row], 0, 1)

        for right in (True, False):
            behind = row if right else last - row

            @pl.when(behind < last)
            def _():
                for c in range(CHUNKS):
                    turn(last - behind - 1, c, right).wait_send()


def local(col_count, row_count, kernel, history, noise_weight, prior_weight):
    sensors, params, steps = kernel.shape
    part_params, vectors, _ = history.shape
    pad = -sensors % 128
    if pad:
        kernel = jnp.pad(kernel, ((0, pad), (0, 0), (0, 0)))
        noise_weight = jnp.pad(noise_weight, ((0, pad), (0, 0)))
        sensors += pad

    table = transform_table(steps)
    th, tl = split_host(table)
    ih, il = split_host(table / steps)
    table_k = jnp.asarray(np.concatenate([th, th, tl], axis=1))
    inverse_t = jnp.asarray(np.concatenate([ih.T, ih.T, il.T], axis=1))
    inverse_f = jnp.asarray(np.concatenate([ih, ih, il], axis=0))

    whole = lambda *shape: pl.BlockSpec(shape, lambda i: (0,) * len(shape))

    hops = CHUNKS * (row_count - 1)
    per_half = sensors // 2 // SENSOR_BLOCK
    anywhere = pl.BlockSpec(memory_space=pl.ANY)
    khat, gathered = pl.pallas_call(
        functools.partial(kernel_transform, row_count),
        grid=(sensors // SENSOR_BLOCK,),
        in_specs=[
            whole(2 * steps, 3 * steps),
            pl.BlockSpec((SENSOR_BLOCK, params, steps), lambda i: (i, 0, 0)),
            whole(part_params, vectors, steps),
        ],
        out_specs=[
            pl.BlockSpec(
                (steps, 1, 2, SENSOR_BLOCK, 2 * params), lambda i: (0, i // per_half, 0, lax.rem(i, per_half), 0)
            ),
            anywhere,
        ],
        out_shape=[
            jax.ShapeDtypeStruct((steps, 2, 2, sensors // 2, 2 * params), bf16),
            jax.ShapeDtypeStruct((row_count, vectors, part_params, steps), f32),
        ],
        scratch_shapes=[
            pltpu.VMEM((vectors, part_params, steps), f32),
            pltpu.VMEM((steps * SENSOR_BLOCK, params), f32),
            pltpu.VMEM((steps * SENSOR_BLOCK, params), f32),
            pltpu.SemaphoreType.DMA,
            pltpu.SemaphoreType.DMA((2, hops)),
            pltpu.SemaphoreType.DMA((2, hops)),
        ],
        compiler_params=pltpu.CompilerParams(
            vmem_limit_bytes=VMEM_LIMIT, collective_id=1, has_side_effects=True
        ),
        cost_estimate=pl.CostEstimate(
            flops=12 * sensors * params * steps * steps,
            bytes_accessed=12 * sensors * params * steps,
            transcendentals=0,
        ),
        name="kernel_transform",
    )(table_k, kernel, history)

    bits = col_count.bit_length() - 1
    total = vectors * steps
    rows = total // 2
    lengths = [rows // 2]
    for level in range(bits - 1):
        lengths += [rows >> (level + 3)] * 2
    phase = steps // FREQ_BLOCK
    gradient = pl.pallas_call(
        functools.partial(normal_operator, bits),
        grid=(4 * phase,),
        in_specs=[
            whole(2 * steps, 3 * steps),
            whole(steps, 6 * steps),
            whole(6 * steps, steps),
            whole(row_count, vectors, part_params, steps),
            whole(sensors, steps),
            pl.BlockSpec(
                (FREQ_BLOCK, 1, 2, sensors // 2, 2 * params),
                lambda i: (lax.rem(i, phase), lax.rem(i // phase, 2), 0, 0, 0),
            ),
        ],
        out_specs=whole(part_params, vectors, steps),
        out_shape=jax.ShapeDtypeStruct((part_params, vectors, steps), f32),
        scratch_shapes=[
            pltpu.VMEM((steps * vectors, params), f32),
            pltpu.VMEM((steps * vectors, params), f32),
            pltpu.VMEM((steps, sensors), f32),
            pltpu.VMEM((steps * vectors, sensors), f32),
            pltpu.VMEM((steps * vectors, sensors), f32),
            pltpu.VMEM((steps * 2 * vectors, params), f32),
            *[pltpu.VMEM((rows, sensors), f32)] * 4,
            pltpu.VMEM((row_count, vectors, part_params, steps), f32),
            pltpu.VMEM((row_count - 1, vectors, part_params, steps), f32),
            pltpu.VMEM((row_count - 1, vectors, part_params, steps), f32),
            *[pltpu.VMEM((length, sensors), f32) for length in lengths] * 2,
            *[pltpu.SemaphoreType.DMA((2 * len(lengths),))] * 4,
            pltpu.SemaphoreType.DMA((2, hops)),
            pltpu.SemaphoreType.DMA((2, hops)),
        ],
        compiler_params=pltpu.CompilerParams(
            vmem_limit_bytes=VMEM_LIMIT, collective_id=0, has_side_effects=True
        ),
        cost_estimate=pl.CostEstimate(
            flops=32 * vectors * sensors * params * steps,
            bytes_accessed=16 * sensors * params * steps,
            transcendentals=0,
        ),
        name="normal_operator",
    )(table_k, inverse_t, inverse_f, gathered, noise_weight, khat)

    return gradient + prior_weight[:, None, None] * history


def solution(mesh):
    in_specs = (
        P("row", "col", None),
        P(("col", "row"), None, None),
        P("row", None),
        P(("col", "row")),
    )
    out_specs = P(("col", "row"), None, None)
    return jax.shard_map(
        functools.partial(local, mesh.shape["col"], mesh.shape["row"]),
        mesh=mesh,
        in_specs=in_specs,
        out_specs=out_specs,
        check_vma=False,
    )
```

```python
import functools
import math

import jax
import jax.numpy as jnp
import ml_dtypes
import numpy as np
from jax import lax
from jax.experimental import pallas as pl
from jax.experimental.pallas import tpu as pltpu
from jax.sharding import PartitionSpec as P

f32 = jnp.float32
bf16 = jnp.bfloat16
VMEM_LIMIT = 60 * 1024 * 1024
SENSOR_BLOCK = 16
FREQ_BLOCK = 32
GROUP = 8


def transform_table(steps):
    freqs = np.arange(steps, dtype=np.int64)[:, None]
    times = np.arange(steps, dtype=np.int64)[None, :]
    phase = ((2 * freqs + 1) * times % (4 * steps)).astype(np.float64) * (math.pi / (2 * steps))
    return np.concatenate([np.cos(phase), -np.sin(phase)], axis=0)


def split_host(table):
    table = table.astype(np.float32)
    high = table.astype(ml_dtypes.bfloat16)
    low = (table - high.astype(np.float32)).astype(ml_dtypes.bfloat16)
    return high, low


def split(value):
    high = value.astype(bf16)
    return high, (value - high.astype(f32)).astype(bf16)


def matmul(lhs, rhs):
    return lax.dot_general(lhs, rhs, (((1,), (0,)), ((), ())), preferred_element_type=f32)


def matmul_nt(lhs, rhs):
    return lax.dot_general(lhs, rhs, (((1,), (1,)), ((), ())), preferred_element_type=f32)


MESH = pl.DeviceIdType.MESH
CHUNKS = 2


def greet_row(me, last, others=0):
    barrier = pltpu.get_barrier_semaphore()

    @pl.when(me > 0)
    def _():
        pl.semaphore_signal(barrier, inc=1, device_id={"row": me - 1}, device_id_type=MESH)

    @pl.when(me < last)
    def _():
        pl.semaphore_signal(barrier, inc=1, device_id={"row": me + 1}, device_id_type=MESH)

    inside = (me > 0) & (me < last)

    @pl.when(inside)
    def _():
        pl.semaphore_wait(barrier, others + 2)

    @pl.when(jnp.logical_not(inside))
    def _():
        pl.semaphore_wait(barrier, others + 1)


def kernel_transform(
    row_count, table_ref, kernel_ref, raw_ref, out_ref, all_ref, hist_ref, real_ref, imag_ref, *sems
):
    own_sem, right_sems, left_sems = sems
    sensors, params, steps = kernel_ref.shape
    grid_step = pl.program_id(0)
    grid_steps = pl.num_programs(0)
    me = lax.axis_index("row")
    last = row_count - 1
    half = hist_ref.shape[0] // CHUNKS
    own = pltpu.make_async_copy(hist_ref, all_ref.at[me], own_sem)

    def hop(h, c, right):
        shard = me - h if right else me + h
        sems = right_sems if right else left_sems
        rows = pl.ds(c * half, half)
        slot = all_ref.at[shard, rows]
        return pltpu.make_async_remote_copy(
            src_ref=hist_ref.at[rows] if h == 0 else slot,
            dst_ref=slot,
            send_sem=sems.at[0, h * CHUNKS + c],
            recv_sem=sems.at[1, h * CHUNKS + c],
            device_id={"row": me + 1 if right else me - 1},
            device_id_type=MESH,
        )

    def sends(h, right):
        return (me < last) & (me >= h) if right else (me > 0) & (me <= last - h)

    def receives(h, right):
        return me >= h + 1 if right else me <= last - h - 1

    def arrival(h, c, right):
        rows = pl.ds(c * half, half)
        slot = all_ref.at[me - 1 - h if right else me + 1 + h, rows]
        sems = right_sems if right else left_sems
        return pltpu.make_async_remote_copy(
            src_ref=slot,
            dst_ref=slot,
            send_sem=sems.at[0, h * CHUNKS + c],
            recv_sem=sems.at[1, h * CHUNKS + c],
            device_id={"row": me - 1 if right else me + 1},
            device_id_type=MESH,
        )

    def wait_arrival(h, c):
        for right in (True, False):

            @pl.when(receives(h, right))
            def _():
                arrival(h, c, right).wait_recv()

    def start_hop(h, c):
        for right in (True, False):

            @pl.when(sends(h, right))
            def _():
                hop(h, c, right).start()

    @pl.when(grid_step == 0)
    def _():
        hist_ref[...] = jnp.swapaxes(raw_ref[...], 0, 1)
        greet_row(me, last)
        for c in range(CHUNKS):
            start_hop(0, c)
        own.start()

    for m in range(CHUNKS * (row_count - 2)):
        h, c = m // CHUNKS, m % CHUNKS
        due = jnp.minimum((m + 1) * grid_steps // (CHUNKS * last) + 1, grid_steps - 1)

        @pl.when(grid_step == due)
        def _():
            wait_arrival(h, c)
            start_hop(h + 1, c)

    for s in range(0, sensors, 2):
        high, low = split(kernel_ref[s : s + 2].reshape(2 * params, steps))
        spec = matmul_nt(table_ref[...], jnp.concatenate([high, low, high], axis=1))
        for j in range(2):
            cols = slice(j * params, (j + 1) * params)
            real_ref[pl.ds(s + j, steps, stride=sensors + 1), :] = spec[:steps, cols]
            imag_ref[pl.ds(s + j, steps, stride=sensors + 1), :] = spec[steps:, cols]

    group = 8

    def emit(i, carry):
        base = pl.multiple_of(i * group * (sensors + 1), group)
        for part, ref in enumerate((real_ref, imag_ref)):
            cols = slice(part * params, (part + 1) * params)
            for g in range(group):
                high, low = split(ref[pl.ds(base + g * (sensors + 1), sensors), :])
                out_ref[i * group + g, 0, 0, :, cols] = high
                out_ref[i * group + g, 0, 1, :, cols] = low
        return carry

    lax.fori_loop(0, steps // group, emit, 0)

    @pl.when(grid_step == grid_steps - 1)
    def _():
        own.wait()
        for c in range(CHUNKS):
            wait_arrival(row_count - 2, c)
        for h in range(row_count - 1):
            for c in range(CHUNKS):
                for right in (True, False):

                    @pl.when(sends(h, right))
                    def _():
                        hop(h, c, right).wait_send()


def col_steps(bits):
    rest = list(range(1, bits))
    return [rest, rest[::-1]]


def rows_of(offset, length):
    return pl.ds(pl.multiple_of(offset, 8), length)


class AllReduce:
    def __init__(self, bits, sensors, time_ref, weighted_ref, noise_ref, recv_refs, send_sem, recv_sem):
        me = lax.axis_index("col")
        self.bits, self.steps, self.sensors = bits, noise_ref.shape[0], sensors
        self.time_ref, self.weighted_ref, self.noise_ref = time_ref, weighted_ref, noise_ref
        self.recv_refs, self.send_sem, self.recv_sem = recv_refs, send_sem, recv_sem
        self.bit_of = [lax.rem(me // 2**b, 2) for b in range(bits)]
        self.partner = [me + (1 - 2 * self.bit_of[b]) * 2**b for b in range(bits)]
        self.orders = col_steps(bits)
        total = time_ref.shape[0]
        self.core_length = total // 2
        self.keep = self.bit_of[0] * self.core_length
        self.give = (1 - self.bit_of[0]) * self.core_length
        length = self.core_length // 2
        self.offsets = [[self.keep, self.keep + length]]
        self.lengths = [length]
        for level in range(bits - 1):
            length //= 2
            self.lengths.append(length)
            self.offsets.append(
                [
                    self.offsets[-1][part] + self.bit_of[self.orders[part][level]] * length
                    for part in range(2)
                ]
            )

    def copy(self, src, dst, sem, bit):
        return pltpu.make_async_remote_copy(
            src_ref=src,
            dst_ref=dst,
            send_sem=self.send_sem.at[sem],
            recv_sem=self.recv_sem.at[sem],
            device_id={"col": self.partner[bit]},
            device_id_type=MESH,
        )

    def stage(self, k):
        levels = self.bits - 1
        if k == 0:
            return [self.copy(self.time_ref.at[rows_of(self.give, self.core_length)], self.recv_refs[0], 0, 0)]
        if k == 2 * levels + 1:
            rows = self.weighted_ref.at[rows_of(self.keep, self.core_length)]
            return [self.copy(rows, rows, 4 * levels + 1, 0)]
        copies = []
        for part in range(2):
            sem = 2 * k - 1 + part
            if k <= levels:
                bit = self.orders[part][k - 1]
                length = self.lengths[k]
                send_at = self.offsets[k - 1][part] + (1 - self.bit_of[bit]) * length
                copies.append(self.copy(self.time_ref.at[rows_of(send_at, length)], self.recv_refs[sem], sem, bit))
            else:
                level = 2 * levels - k
                bit = self.orders[part][level]
                rows = self.weighted_ref.at[rows_of(self.offsets[level + 1][part], self.lengths[level + 1])]
                copies.append(self.copy(rows, rows, sem, bit))
        return copies

    def start(self, k):
        for copy in self.stage(k):
            copy.start()

    def finish(self, k):
        levels = self.bits - 1
        copies = self.stage(k)
        for part in range(2):
            if part < len(copies):
                copies[part].wait()
            if k <= levels:
                length = self.lengths[k]
                rows = rows_of(self.offsets[k][part], length)
                if k == 0:
                    self.time_ref[rows, :] += self.recv_refs[0][part * length : (part + 1) * length, :]
                else:
                    self.time_ref[rows, :] += self.recv_refs[2 * k - 1 + part][...]
            if k == levels:
                piece = min(length, self.steps)
                for j in range(length // piece):
                    at = self.offsets[k][part] + j * piece
                    noise = self.noise_ref[rows_of(lax.rem(at, self.steps), piece), :][:, self.sensors]
                    noise = jnp.concatenate([noise, noise], axis=1)
                    self.weighted_ref[rows_of(at, piece), :] = self.time_ref[rows_of(at, piece), :] * noise


def normal_operator(
    bits,
    table_k_ref,
    inverse_t_ref,
    inverse_f_ref,
    hist_ref,
    weights_ref,
    khat_ref,
    out_ref,
    hreal_ref,
    himag_ref,
    noise_ref,
    spec_a_ref,
    spec_b_ref,
    grad_ref,
    time_a_ref,
    time_b_ref,
    weighted_a_ref,
    weighted_b_ref,
    partial_ref,
    from_left_ref,
    from_right_ref,
    *comm,
):
    sems = comm[-6:]
    right_sems, left_sems = sems[4:]
    recv_count = (len(comm) - 6) // 2
    step = pl.program_id(0)
    phase = pl.num_programs(0) // 4
    blocks, vectors, part_params, steps = hist_ref.shape
    params = blocks * part_params
    freq_block, _, _, half, _ = khat_ref.shape
    pairs = vectors // 2
    lanes = 2 * half
    spec_refs = (spec_a_ref, spec_b_ref)
    time_refs = (time_a_ref, time_b_ref)
    weighted_refs = (weighted_a_ref, weighted_b_ref)
    reduces = [
        AllReduce(
            bits, slice(h * half, (h + 1) * half), time_refs[h], weighted_refs[h], noise_ref,
            comm[h * recv_count : (h + 1) * recv_count], sems[2 * h], sems[2 * h + 1],
        )
        for h in range(2)
    ]
    stages = 2 * bits

    @pl.when(step == 0)
    def _():
        barrier = pltpu.get_barrier_semaphore()
        for b in range(bits):
            pl.semaphore_signal(barrier, inc=1, device_id={"col": reduces[0].partner[b]}, device_id_type=MESH)
        greet_row(lax.axis_index("row"), blocks - 1, bits)

        noise_ref[...] = weights_ref[...].T
        for r in range(0, vectors, 2):
            hist = jnp.concatenate([hist_ref[:, r + j].reshape(params, steps) for j in range(2)], axis=0)
            high, low = split(hist)
            spec = matmul_nt(table_k_ref[...], jnp.concatenate([high, low, high], axis=1))
            for j in range(2):
                cols = slice(j * params, (j + 1) * params)
                rows = pl.ds(j * pairs + r // 2, steps, stride=vectors + 1)
                hreal_ref[rows, :] = spec[:steps, cols]
                himag_ref[rows, :] = spec[steps:, cols]

    def grouped(product):
        for first in range(0, freq_block, GROUP):
            stores = [product(first + i) for i in range(GROUP)]
            for ref, rows, value in sum(stores, []):
                ref[rows, :] = value

    def forward(h):
        def product(i):
            f = lax.rem(step, phase) * freq_block + i
            rows = pl.ds(f * (vectors + 1), vectors)
            real, imag = hreal_ref[rows, :], himag_ref[rows, :]
            top, bottom = jnp.concatenate([real, -imag], axis=1), jnp.concatenate([imag, real], axis=1)
            both = jnp.concatenate([top[:pairs], bottom[:pairs], top[pairs:], bottom[pairs:]], axis=0)
            lhs = jnp.concatenate(split(both), axis=0)
            res = matmul_nt(lhs, khat_ref[i, 0].reshape(lanes, 2 * params))
            high, low = res[: 2 * vectors], res[2 * vectors :]
            data = high[:, :half] + (high[:, half:] + low[:, :half])
            return [(spec_refs[h], rows, jnp.concatenate([data[:vectors], data[vectors:]], axis=1))]

        grouped(product)

    def to_time(h, pair):
        spec_ref = spec_refs[h]
        spec = jnp.concatenate(
            [
                jnp.concatenate(
                    [spec_ref[pl.ds(part * pairs + pair + j, steps, stride=vectors + 1), :] for j in range(2)],
                    axis=1,
                )
                for part in range(2)
            ],
            axis=0,
        )
        high, low = split(spec)
        times = matmul(inverse_t_ref[...], jnp.concatenate([high, low, high], axis=0))
        for j in range(2):
            time_refs[h][rows_of((pair + j) * steps, steps), :] = times[:, j * lanes : (j + 1) * lanes]

    def to_spectrum(h, pair):
        weighted = [weighted_refs[h][rows_of((pair + j) * steps, steps), :] for j in range(2)]
        high, low = split(jnp.concatenate(weighted, axis=1))
        spec = matmul(table_k_ref[...], jnp.concatenate([high, low, high], axis=0))
        for j in range(2):
            cols = slice(j * lanes, (j + 1) * lanes)
            spec_refs[h][pl.ds(pair + j, steps, stride=vectors + 1), :] = spec[:steps, cols]
            spec_refs[h][pl.ds(pairs + pair + j, steps, stride=vectors + 1), :] = spec[steps:, cols]

    def over_pairs(body, h, first):
        def one(j, carry):
            body(h, first + 2 * j)
            return carry

        lax.fori_loop(0, pairs // 4, one, 0)

    def begin(h):
        reduce = reduces[h]
        over_pairs(to_time, h, (1 - reduce.bit_of[0]) * (pairs // 2))
        reduce.start(0)
        over_pairs(to_time, h, reduce.bit_of[0] * (pairs // 2))

    def end(h):
        reduce = reduces[h]
        over_pairs(to_spectrum, h, reduce.bit_of[0] * (pairs // 2))
        reduce.finish(stages - 1)
        over_pairs(to_spectrum, h, (1 - reduce.bit_of[0]) * (pairs // 2))

    shares = [1.9] + [1 + 2.6 / 2**level for level in range(bits - 1)]
    shares = shares + shares[::-1]

    def events(h, base):
        done = 0.0
        for k in range(1, stages):
            done += shares[k - 1]

            @pl.when(step == base + jnp.minimum((int(1024 * done / sum(shares)) * phase + 1023) // 1024, phase - 1))
            def _():
                reduces[h].finish(k - 1)
                reduces[h].start(k)

    def backward(h):
        def product(i):
            f = lax.rem(step, phase) * freq_block + i
            base = f * (2 * vectors + 1)
            mine = spec_refs[h][pl.ds(f * (vectors + 1), vectors), :]
            swapped = jnp.concatenate([mine[:, half:], mine[:, :half]], axis=1)
            left = lax.broadcasted_iota(jnp.int32, mine.shape, 1) < half
            both = jnp.concatenate([jnp.where(left, mine, swapped), jnp.where(left, swapped, mine)], axis=0)
            high, low = split(both)
            left = lax.broadcasted_iota(jnp.int32, both.shape, 1) < half
            low = jnp.where(left, low.astype(f32), 0.0).astype(bf16)
            res = matmul(jnp.concatenate([high, low], axis=0), khat_ref[i, 0].reshape(lanes, 2 * params))
            res = res[: 2 * vectors] + res[2 * vectors :]
            real = jnp.concatenate([res[:pairs], res[vectors : vectors + pairs]], axis=0)
            imag = jnp.concatenate([res[pairs:vectors], res[vectors + pairs :]], axis=0)
            values = [real[:, :params] + imag[:, params:], imag[:, :params] - real[:, params:]]
            rows = [pl.ds(base, vectors), pl.ds(base + vectors, vectors)]
            if h == 1:
                values = [value + grad_ref[at, :] for value, at in zip(values, rows)]
            return [(grad_ref, at, value) for value, at in zip(values, rows)]

        grouped(product)

    @pl.when(step < phase)
    def _():
        forward(0)

    @pl.when(step == phase - 1)
    def _():
        begin(0)

    events(0, phase)

    @pl.when((step >= phase) & (step < 2 * phase))
    def _():
        forward(1)

    @pl.when(step == 2 * phase - 1)
    def _():
        begin(1)
        end(0)

    events(1, 2 * phase)

    @pl.when((step >= 2 * phase) & (step < 3 * phase))
    def _():
        backward(0)

    @pl.when(step == 3 * phase - 1)
    def _():
        end(1)

    @pl.when(step >= 3 * phase)
    def _():
        backward(1)

    @pl.when(step == 4 * phase - 1)
    def _():
        chunk = vectors // CHUNKS
        last = blocks - 1
        row = lax.axis_index("row")

        def to_gradient(r):
            spec = jnp.concatenate(
                [
                    jnp.concatenate(
                        [
                            grad_ref[pl.ds(part * vectors + j * pairs + r // 2, steps, stride=2 * vectors + 1), :]
                            for part in range(2)
                        ],
                        axis=0,
                    ).T
                    for j in range(2)
                ],
                axis=0,
            )
            high, low = split(spec)
            times = matmul(jnp.concatenate([high, low, high], axis=1), inverse_f_ref[...])
            for j in range(2):
                partial_ref[:, r + j] = times[j * params : (j + 1) * params].reshape(blocks, part_params, steps)

        def turn(q, c, right, arriving=False):
            rows = pl.ds(c * chunk, chunk)
            sems = right_sems if right else left_sems
            landing = from_left_ref if right else from_right_ref
            return pltpu.make_async_remote_copy(
                src_ref=partial_ref.at[last - q if right else q, rows],
                dst_ref=landing.at[q, rows],
                send_sem=sems.at[0, q * CHUNKS + c],
                recv_sem=sems.at[1, q * CHUNKS + c],
                device_id={"row": row + 1 if right != arriving else row - 1},
                device_id_type=MESH,
            )

        def step_of_line(t, c):
            rows = pl.ds(c * chunk, chunk)
            for right in (True, False):
                behind = row if right else last - row
                q = t - behind
                landing = from_left_ref if right else from_right_ref

                @pl.when((q >= 0) & (q <= last - behind) & (behind > 0))
                def _():
                    turn(q, c, right, arriving=True).wait_recv()
                    shard = last - q if right else q
                    partial_ref[shard, rows] += landing[q, rows]

                @pl.when((q >= 0) & (q < last - behind))
                def _():
                    @pl.when(q >= 1)
                    def _():
                        turn(q - 1, c, right).wait_send()

                    turn(q, c, right).start()

        for c in range(CHUNKS):

            def gradient_body(j, carry):
                to_gradient(c * chunk + 2 * j)
                return carry

            lax.fori_loop(0, chunk // 2, gradient_body, 0)
            step_of_line(0, c)

        def line_body(t, carry):
            for c in range(CHUNKS):
                step_of_line(t, c)
            return carry

        lax.fori_loop(1, blocks, line_body, 0)
        out_ref[...] = jnp.swapaxes(partial_ref[row], 0, 1)

        for right in (True, False):
            behind = row if right else last - row

            @pl.when(behind < last)
            def _():
                for c in range(CHUNKS):
                    turn(last - behind - 1, c, right).wait_send()


def local(col_count, row_count, kernel, history, noise_weight, prior_weight):
    sensors, params, steps = kernel.shape
    part_params, vectors, _ = history.shape
    pad = -sensors % 128
    if pad:
        kernel = jnp.pad(kernel, ((0, pad), (0, 0), (0, 0)))
        noise_weight = jnp.pad(noise_weight, ((0, pad), (0, 0)))
        sensors += pad

    table = transform_table(steps)
    th, tl = split_host(table)
    ih, il = split_host(table / steps)
    table_k = jnp.asarray(np.concatenate([th, th, tl], axis=1))
    inverse_t = jnp.asarray(np.concatenate([ih.T, ih.T, il.T], axis=1))
    inverse_f = jnp.asarray(np.concatenate([ih, ih, il], axis=0))

    whole = lambda *shape: pl.BlockSpec(shape, lambda i: (0,) * len(shape))

    hops = CHUNKS * (row_count - 1)
    per_half = sensors // 2 // SENSOR_BLOCK
    anywhere = pl.BlockSpec(memory_space=pl.ANY)
    khat, gathered = pl.pallas_call(
        functools.partial(kernel_transform, row_count),
        grid=(sensors // SENSOR_BLOCK,),
        in_specs=[
            whole(2 * steps, 3 * steps),
            pl.BlockSpec((SENSOR_BLOCK, params, steps), lambda i: (i, 0, 0)),
            whole(part_params, vectors, steps),
        ],
        out_specs=[
            pl.BlockSpec(
                (steps, 1, 2, SENSOR_BLOCK, 2 * params), lambda i: (0, i // per_half, 0, lax.rem(i, per_half), 0)
            ),
            anywhere,
        ],
        out_shape=[
            jax.ShapeDtypeStruct((steps, 2, 2, sensors // 2, 2 * params), bf16),
            jax.ShapeDtypeStruct((row_count, vectors, part_params, steps), f32),
        ],
        scratch_shapes=[
            pltpu.VMEM((vectors, part_params, steps), f32),
            pltpu.VMEM(((steps + 1) * (SENSOR_BLOCK + 1), params), f32),
            pltpu.VMEM(((steps + 1) * (SENSOR_BLOCK + 1), params), f32),
            pltpu.SemaphoreType.DMA,
            pltpu.SemaphoreType.DMA((2, hops)),
            pltpu.SemaphoreType.DMA((2, hops)),
        ],
        compiler_params=pltpu.CompilerParams(
            vmem_limit_bytes=VMEM_LIMIT, collective_id=1, has_side_effects=True
        ),
        cost_estimate=pl.CostEstimate(
            flops=12 * sensors * params * steps * steps,
            bytes_accessed=12 * sensors * params * steps,
            transcendentals=0,
        ),
        name="kernel_transform",
    )(table_k, kernel, history)

    bits = col_count.bit_length() - 1
    total = vectors * steps
    rows = total // 2
    lengths = [rows // 2]
    for level in range(bits - 1):
        lengths += [rows >> (level + 3)] * 2
    phase = steps // FREQ_BLOCK
    gradient = pl.pallas_call(
        functools.partial(normal_operator, bits),
        grid=(4 * phase,),
        in_specs=[
            whole(2 * steps, 3 * steps),
            whole(steps, 6 * steps),
            whole(6 * steps, steps),
            whole(row_count, vectors, part_params, steps),
            whole(sensors, steps),
            pl.BlockSpec(
                (FREQ_BLOCK, 1, 2, sensors // 2, 2 * params),
                lambda i: (lax.rem(i, phase), lax.rem(i // phase, 2), 0, 0, 0),
            ),
        ],
        out_specs=whole(part_params, vectors, steps),
        out_shape=jax.ShapeDtypeStruct((part_params, vectors, steps), f32),
        scratch_shapes=[
            pltpu.VMEM(((steps + 1) * (vectors + 1), params), f32),
            pltpu.VMEM(((steps + 1) * (vectors + 1), params), f32),
            pltpu.VMEM((steps, sensors), f32),
            pltpu.VMEM(((steps + 1) * (vectors + 1), sensors), f32),
            pltpu.VMEM(((steps + 1) * (vectors + 1), sensors), f32),
            pltpu.VMEM(((steps + 1) * (2 * vectors + 1), params), f32),
            *[pltpu.VMEM((rows, sensors), f32)] * 4,
            pltpu.VMEM((row_count, vectors, part_params, steps), f32),
            pltpu.VMEM((row_count - 1, vectors, part_params, steps), f32),
            pltpu.VMEM((row_count - 1, vectors, part_params, steps), f32),
            *[pltpu.VMEM((length, sensors), f32) for length in lengths] * 2,
            *[pltpu.SemaphoreType.DMA((2 * len(lengths),))] * 4,
            pltpu.SemaphoreType.DMA((2, hops)),
            pltpu.SemaphoreType.DMA((2, hops)),
        ],
        compiler_params=pltpu.CompilerParams(
            vmem_limit_bytes=VMEM_LIMIT, collective_id=0, has_side_effects=True
        ),
        cost_estimate=pl.CostEstimate(
            flops=32 * vectors * sensors * params * steps,
            bytes_accessed=16 * sensors * params * steps,
            transcendentals=0,
        ),
        name="normal_operator",
    )(table_k, inverse_t, inverse_f, gathered, noise_weight, khat)

    return gradient + prior_weight[:, None, None] * history


def solution(mesh):
    in_specs = (
        P("row", "col", None),
        P(("col", "row"), None, None),
        P("row", None),
        P(("col", "row")),
    )
    out_specs = P(("col", "row"), None, None)
    return jax.shard_map(
        functools.partial(local, mesh.shape["col"], mesh.shape["row"]),
        mesh=mesh,
        in_specs=in_specs,
        out_specs=out_specs,
        check_vma=False,
    )
```
